128 devices in a mesh: gx: 8 (over z, core), gy: 16 (over x, y).
Axes of the slice: x: 4, y: 4, z: 4, core: 2. Of those that a mesh axis runs over, the one named last changes fastest.
Arguments:
- grad_out: bfloat16 [1048576, 128], P(('gx', 'gy')), may hold values from -6 to 6
- preact: bfloat16 [1048576, 128], P(('gx', 'gy')), may hold values from -6 to 6
- features: bfloat16 [1048576, 128], P(('gx', 'gy')), may hold values from -6 to 6
- neighbour_mean: bfloat16 [1048576, 128], P(('gx', 'gy')), may hold values from -6 to 6
- w_self: bfloat16 [128, 128], replicated, may hold values from -0.5 to 0.5
- w_neigh: bfloat16 [128, 128], replicated, may hold values from -0.5 to 0.5
- degrees: int32 [1048576], P(('gx', 'gy')), may hold values from 8 to 63
- tile_values: bfloat16 [49152, 128, 128], P(('gx', 'gy')), may hold values from 0.0099487305 to 1
- tile_list: int32 [128, 2, 384], P(('gx', 'gy')), may hold values from 0 to 8191, as said below
- send_counts: int32 [128, 128], P(('gx', 'gy')), may hold values from 0 to 3, as said below
Outputs:
- grad_features: bfloat16 [1048576, 128], P(('gx', 'gy'))
- grad_neighbour: bfloat16 [1048576, 128], P(('gx', 'gy'))
- grad_w_self: float32 [128, 128], replicated
- grad_w_neigh: float32 [128, 128], replicated
The draws below stay inside these ranges and needn't reach their ends.
Inputs may be any that keep to these rules, and one draw needn't show every extreme that they name: `tile_list`: entry [i, 0, s] is a block row of device i's own range (i * 64 to i * 64 + 63); entry [i, 1, s] is a block column of the range of device s // 3. `send_counts`: every device uses all 3 slots for its own range; in every draw one device receives 3 used slots from every device.
All inputs are finite; a program needn't handle non-finite values.
Results may differ from the reference program's by a relative error of at most 0.0028.
Values may be sent and summed in bfloat16 or wider, within the bound.
No kernel may reach another device: no remote copies, remote signals or barrier semaphores. Data moves between devices by JAX's collectives and lax.ppermute only.
A program may use at most 192 MiB of HBM per device.

```python
import math
import jax
import jax.numpy as jnp
from jax import lax

H = 128
BLOCK = 128
NB_DEV = 64
CAP = 3
NODES = 1048576
DEVICES = 128


def draw_tile_list(key, part):
    key = jax.random.fold_in(key, 11)
    key_rows, key_cols = jax.random.split(key)
    sender = jnp.arange(DEVICES, dtype=jnp.int32)[:, None]
    slot_ids = jnp.arange(DEVICES * CAP, dtype=jnp.int32)[None, :]
    block_rows = sender * NB_DEV + jax.random.randint(key_rows, (DEVICES, DEVICES * CAP), 0, NB_DEV)
    block_cols = slot_ids // CAP * NB_DEV + jax.random.randint(key_cols, (DEVICES, DEVICES * CAP), 0, NB_DEV)
    return jnp.stack([block_rows, block_cols], axis=1).astype(jnp.int32)


def draw_send_counts(key, part):
    key = jax.random.fold_in(key, 23)
    key_level, key_count, key_target = jax.random.split(key, 3)
    level = jax.random.randint(key_level, (DEVICES, 1), 1, CAP + 1)
    counts = jnp.minimum(jax.random.randint(key_count, (DEVICES, DEVICES), 0, CAP + 1), level)
    target = jax.random.randint(key_target, (), 0, DEVICES)
    column_ids = jnp.arange(DEVICES, dtype=jnp.int32)
    counts = jnp.where(column_ids[None, :] == target, CAP, counts)
    counts = jnp.where(column_ids[None, :] == column_ids[:, None], CAP, counts)
    return counts.astype(jnp.int32)


def with_ends(drawn, stream_key, least, high):
    shape = drawn.shape
    spot = [jax.random.randint(jax.random.fold_in(stream_key, axis), (), 0, shape[axis]) for axis in range(len(shape))]
    drawn = drawn.at[tuple(spot)].set(least)
    longest = shape.index(max(shape))
    spot[longest] = (spot[longest] + 1) % shape[longest]
    return drawn.at[tuple(spot)].set(high)


def level_of(rng, dims, pieces, least, high):
    gain = 1.0
    for axis_at, shards_of in pieces:
        steps = jax.random.uniform(jax.random.fold_in(jax.random.fold_in(rng, 6), axis_at), (shards_of,), jnp.float32, least / len(pieces), high / len(pieces))
        gain = gain * jnp.repeat(jnp.exp(steps), dims[axis_at] // shards_of).reshape((-1,) + (1,) * (len(dims) - 1 - axis_at))
    return gain


def bell_draw(stream_key, shape, scale, bound, cuts=(), kind=jnp.bfloat16):
    values = scale * jax.random.normal(stream_key, shape, jnp.float32)
    if cuts:
        values = values * level_of(stream_key, shape, cuts, -0.22, 0.18)
    return jnp.clip(values, -bound, bound).astype(kind)


def setup_inputs(seed: int = 0) -> dict:
    arg_keys = jax.random.split(jax.random.key(seed), 11)
    return {
        "grad_out": bell_draw(arg_keys[0], (NODES, H), 1.0, 6.0, ((0, 128),)),
        "preact": bell_draw(arg_keys[1], (NODES, H), 1.0, 6.0, ((0, 128),)),
        "features": bell_draw(arg_keys[2], (NODES, H), 1.0, 6.0, ((0, 128),)),
        "neighbour_mean": bell_draw(arg_keys[3], (NODES, H), 1.0, 6.0, ((0, 128),)),
        "w_self": bell_draw(arg_keys[4], (H, H), H ** -0.5, 0.5),
        "w_neigh": bell_draw(arg_keys[5], (H, H), H ** -0.5, 0.5),
        "degrees": with_ends(jax.random.randint(arg_keys[6], (NODES,), 8, 64), jax.random.fold_in(arg_keys[6], 1), 8, 63).astype(jnp.int32),
        "tile_values": jnp.clip(jnp.exp(math.log(1.0) - 4.61031033 * jax.random.uniform(arg_keys[7], (DEVICES * DEVICES * CAP, BLOCK, BLOCK), jnp.float32) ** level_of(arg_keys[7], (DEVICES * DEVICES * CAP, BLOCK, BLOCK), ((0, 128),), -0.2, 0.2)), 0.0099487305, 1.0).astype(jnp.bfloat16),
        "tile_list": draw_tile_list(jax.random.fold_in(arg_keys[10], 71), 0),
        "send_counts": draw_send_counts(jax.random.fold_in(arg_keys[10], 71), 0),
    }


def reference(grad_out, preact, features, neighbour_mean, w_self, w_neigh, degrees, tile_values, tile_list, send_counts):
    relu_grad = jnp.where(preact > 0, grad_out, jnp.zeros_like(grad_out))
    neigh_grad = jnp.dot(relu_grad, w_neigh.T, preferred_element_type=jnp.float32)
    grad_neighbour = neigh_grad.astype(jnp.bfloat16)
    scaled_grad = (neigh_grad / degrees.astype(jnp.float32)[:, None]).astype(jnp.bfloat16)
    row_blocks = scaled_grad.reshape(DEVICES * NB_DEV, BLOCK, H)
    slot_count = DEVICES * CAP
    tile_sets = tile_values.reshape(DEVICES, slot_count, BLOCK, BLOCK)
    slot_ids = jnp.arange(slot_count, dtype=jnp.int32)
    slot_peer = slot_ids // CAP
    slot_within = slot_ids % CAP

    def add_sender(accumulated, sender_item):
        tile_set, tile_rows, counts = sender_item
        picked_rows = row_blocks[tile_rows[0]]
        slot_terms = jnp.einsum('sij,sik->sjk', tile_set.astype(jnp.float32), picked_rows.astype(jnp.float32))
        slot_valid = slot_within < counts[slot_peer]
        slot_terms = jnp.where(slot_valid[:, None, None], slot_terms, jnp.zeros_like(slot_terms)).astype(jnp.bfloat16)
        accumulated = accumulated.at[tile_rows[1]].add(slot_terms.astype(accumulated.dtype))
        return (accumulated, None)
    accumulated = jnp.zeros((DEVICES * NB_DEV, BLOCK, H), jnp.float32)
    accumulated, _ = lax.scan(add_sender, accumulated, (tile_sets, tile_list, send_counts))
    self_grad = jnp.dot(relu_grad, w_self.T, preferred_element_type=jnp.float32)
    grad_features = (self_grad + accumulated.reshape(DEVICES * NB_DEV * BLOCK, H)).astype(jnp.bfloat16)
    grad_scale = 1.0 / math.sqrt(DEVICES * NB_DEV * BLOCK)
    grad_w_self = jnp.dot(features.T, relu_grad, preferred_element_type=jnp.float32) * grad_scale
    grad_w_neigh = jnp.dot(neighbour_mean.T, relu_grad, preferred_element_type=jnp.float32) * grad_scale
    return (grad_features, grad_neighbour, grad_w_self, grad_w_neigh)
```

```python
import functools
import math

import jax
import jax.numpy as jnp
from jax import lax
from jax.experimental import pallas as pl
from jax.experimental.pallas import tpu as pltpu
from jax.sharding import PartitionSpec as P

BF16 = jnp.bfloat16
F32 = jnp.float32
AXES = ("gx", "gy")
NT = (((1,), (1,)), ((), ()))
TN = (((0,), (0,)), ((), ()))
VMEM_LIMIT = 50 * 1024 * 1024
EXTRA = 8


def dot(a, b, dims=(((1,), (0,)), ((), ()))):
    return lax.dot_general(a, b, dims, preferred_element_type=F32)


def params():
    return pltpu.CompilerParams(
        dimension_semantics=("arbitrary",), vmem_limit_bytes=VMEM_LIMIT
    )


def cost(flops, nbytes):
    return pl.CostEstimate(flops=flops, bytes_accessed=nbytes, transcendentals=0)


def relu_of(grad_ref, pre_ref):
    grad = grad_ref[...]
    return jnp.where(pre_ref[...] > 0, grad, jnp.zeros_like(grad))


def node_kernel(scale, grad_ref, pre_ref, feat_ref, mean_ref, wn_ref, deg_ref, gn_ref, st_ref, gw_ref):
    width = wn_ref.shape[0]
    blocks = st_ref.shape[0]
    relu = relu_of(grad_ref, pre_ref)
    relu_t = relu.T
    wn = wn_ref[...]
    gn_ref[...] = dot(relu, wn, NT).astype(BF16)
    ngt = dot(wn, relu_t)
    inv = 1.0 / deg_ref[...].astype(F32)
    block = deg_ref.shape[1]
    for b in range(blocks):
        st_ref[b] = (ngt[:, b * block : (b + 1) * block] * inv[b : b + 1, :]).astype(BF16)

    @pl.when(pl.program_id(0) == 0)
    def _():
        gw_ref[...] = jnp.zeros_like(gw_ref)

    gw_ref[:, :width] += dot(relu_t, feat_ref[...]) * scale
    gw_ref[:, width:] += dot(relu_t, mean_ref[...]) * scale


def node_stage(grad_out, preact, features, mean, w_neigh, degrees, block, scale):
    rows, width = grad_out.shape
    tile = 8 * block
    steps = rows // tile
    node = pl.BlockSpec((tile, width), lambda i: (i, 0))
    return pl.pallas_call(
        functools.partial(node_kernel, scale),
        grid=(steps,),
        in_specs=[
            node,
            node,
            node,
            node,
            pl.BlockSpec((width, width), lambda i: (0, 0)),
            pl.BlockSpec((8, block), lambda i: (i, 0)),
        ],
        out_specs=[
            node,
            pl.BlockSpec((8, width, block), lambda i: (i, 0, 0)),
            pl.BlockSpec((width, 2 * width), lambda i: (0, 0)),
        ],
        out_shape=[
            jax.ShapeDtypeStruct((rows, width), BF16),
            jax.ShapeDtypeStruct((rows // block, width, block), BF16),
            jax.ShapeDtypeStruct((width, 2 * width), F32),
        ],
        compiler_params=params(),
        cost_estimate=cost(8 * rows * width * width, 14 * rows * width),
        name="node_stage",
    )(grad_out, preact, features, mean, w_neigh, degrees.reshape(rows // block, block))


def hi_lo_rows(a, b, tail):
    width = a.shape[1]
    row = lax.broadcasted_iota(jnp.int32, (EXTRA, width), 0)
    a = jnp.broadcast_to(a, (EXTRA, width))
    b = jnp.broadcast_to(b, (EXTRA, width))
    a_hi = a.astype(BF16).astype(F32)
    b_hi = b.astype(BF16).astype(F32)
    out = jnp.where(row == 0, a_hi, jnp.where(row == 1, b_hi, jnp.where(row == 2, a - a_hi, b - b_hi)))
    return jnp.where(row < 4, out, jnp.where(row == 4, tail, 0.0))


def term_kernel(slots, capacity, group, transposed, list_ref, count_ref, st_ref, tile_ref, *rest):
    blocks = st_ref.shape[0]
    width = st_ref.shape[1]
    step = pl.program_id(0)
    *gw_ref, out_ref = rest
    if gw_ref:
        share = gw_ref[0][pl.ds(pl.multiple_of(step * group, group), group), :]
    for d in range(group):
        dest = step * group + d
        for k, slot in enumerate(slots):
            s = dest * capacity + slot
            row = lax.rem(list_ref[0, s], blocks)
            rows_t = st_ref[row]
            if transposed:
                term = dot(rows_t, tile_ref[d, k])
            else:
                term = dot(tile_ref[d, k], rows_t, (((0,), (1,)), ((), ())))
            keep = slot < count_ref[dest]
            out_ref[d, k * width : (k + 1) * width, :] = jnp.where(keep, term, 0.0).astype(BF16)
        base = len(slots) * width
        if gw_ref:
            lane = lax.broadcasted_iota(jnp.int32, (1, width), 1)
            cols = jnp.zeros((1, width), jnp.int32)
            for c in range(capacity):
                cols = jnp.where(lane == c, lax.rem(list_ref[1, dest * capacity + c], blocks), cols)
            a = share[d : d + 1, :width]
            b = share[d : d + 1, width:]
            extra = hi_lo_rows(a, b, jnp.broadcast_to(cols.astype(F32), (EXTRA, width)))
            out_ref[d, base : base + EXTRA, :] = extra.astype(BF16)
        else:
            out_ref[d, base : base + EXTRA, :] = jnp.zeros((EXTRA, width), BF16)


def terms(tile_list, counts, st, tiles, slots, transposed, gw=None, group=8):
    peers, capacity, block, _ = tiles.shape
    blocks, width, _ = st.shape
    n = len(slots)
    at = slots[0] // n
    rows = n * block + EXTRA
    in_specs = [
        pl.BlockSpec((blocks, width, block), lambda i, *_: (0, 0, 0)),
        pl.BlockSpec((group, n, block, block), lambda i, *_: (i, at, 0, 0)),
    ]
    args = [st, tiles]
    if gw is not None:
        in_specs.append(pl.BlockSpec(gw.shape, lambda i, *_: (0, 0)))
        args.append(gw)
    return pl.pallas_call(
        functools.partial(term_kernel, slots, capacity, group, transposed),
        grid_spec=pltpu.PrefetchScalarGridSpec(
            num_scalar_prefetch=2,
            grid=(peers // group,),
            in_specs=in_specs,
            out_specs=pl.BlockSpec((group, rows, width), lambda i, *_: (i, 0, 0)),
        ),
        out_shape=jax.ShapeDtypeStruct((peers, rows, width), BF16),
        compiler_params=params(),
        cost_estimate=cost(2 * peers * n * block**3, 4 * peers * n * block * block),
        name="terms",
    )(tile_list, counts, *args)


def first_sum_kernel(group, cols_ref, got_ref, grad_ref, pre_ref, ws_ref, out_ref, acc):
    step = pl.program_id(0)
    steps = pl.num_programs(0)
    block = acc.shape[1]

    @pl.when(step == 0)
    def _():
        acc[...] = jnp.zeros_like(acc)

    for d in range(group):
        col = cols_ref[2, step * group + d]
        acc[col] += got_ref[d, :block, :].astype(F32)

    @pl.when(step == steps - 1)
    def _():
        @pl.loop(0, acc.shape[0])
        def _(b):
            at = pl.ds(pl.multiple_of(b * block, block), block)
            relu = relu_of(grad_ref.at[at], pre_ref.at[at])
            out_ref[b] = acc[b].T + dot(relu, ws_ref[...], NT)


def first_sum(cols, got, grad_out, preact, w_self, group=8):
    peers, rows, width = got.shape
    nodes = grad_out.shape[0]
    block = rows - EXTRA
    blocks = nodes // block
    whole = pl.BlockSpec((nodes, width), lambda i, *_: (0, 0))
    return pl.pallas_call(
        functools.partial(first_sum_kernel, group),
        grid_spec=pltpu.PrefetchScalarGridSpec(
            num_scalar_prefetch=1,
            grid=(peers // group,),
            in_specs=[
                pl.BlockSpec((group, rows, width), lambda i, *_: (i, 0, 0)),
                whole,
                whole,
                pl.BlockSpec((width, width), lambda i, *_: (0, 0)),
            ],
            out_specs=pl.BlockSpec((blocks, block, width), lambda i, *_: (0, 0, 0)),
            scratch_shapes=[pltpu.VMEM((blocks, block, width), F32)],
        ),
        out_shape=jax.ShapeDtypeStruct((blocks, block, width), F32),
        compiler_params=params(),
        cost_estimate=cost(2 * nodes * width * width, 2 * peers * rows * width + 8 * nodes * width),
        name="first_sum",
    )(cols, got, grad_out, preact, w_self)


def last_sum_kernel(group, slots, cols_ref, got_ref, base_ref, out_ref, gs_ref, gn_ref, acc, gw, sem):
    step = pl.program_id(0)
    steps = pl.num_programs(0)
    block, width = acc.shape[1:]
    load = pltpu.make_async_copy(base_ref, acc, sem)

    @pl.when(step == 0)
    def _():
        load.start()
        load.wait()

    shares = []
    for d in range(group):
        src = step * group + d
        for k in range(slots):
            col = cols_ref[k, src]
            acc[col] += got_ref[d, k * block : (k + 1) * block, :].astype(F32)
        extra = got_ref[d, slots * block : slots * block + EXTRA, :].astype(F32)
        shares.append(extra[:2] + extra[2:4])
    at = pl.ds(pl.multiple_of(step * group, group), group)
    gw[at, :width] = jnp.concatenate([share[:1] for share in shares], axis=0)
    gw[at, width:] = jnp.concatenate([share[1:] for share in shares], axis=0)

    @pl.when(step == steps - 1)
    def _():
        @pl.loop(0, acc.shape[0])
        def _(b):
            out_ref[b] = acc[b].astype(BF16)

        gs_ref[...] = gw[:, :width].T
        gn_ref[...] = gw[:, width:].T


def last_sum(cols, got, base, slots, group=8):
    peers, rows, width = got.shape
    blocks, block, _ = base.shape
    square = pl.BlockSpec((width, width), lambda i, *_: (0, 0))
    return pl.pallas_call(
        functools.partial(last_sum_kernel, group, slots),
        grid_spec=pltpu.PrefetchScalarGridSpec(
            num_scalar_prefetch=1,
            grid=(peers // group,),
            in_specs=[
                pl.BlockSpec((group, rows, width), lambda i, *_: (i, 0, 0)),
                pl.BlockSpec(memory_space=pl.ANY),
            ],
            out_specs=[
                pl.BlockSpec((blocks, block, width), lambda i, *_: (0, 0, 0)),
                square,
                square,
            ],
            scratch_shapes=[
                pltpu.VMEM((blocks, block, width), F32),
                pltpu.VMEM((width, 2 * width), F32),
                pltpu.SemaphoreType.DMA,
            ],
        ),
        out_shape=[
            jax.ShapeDtypeStruct((blocks, block, width), BF16),
            jax.ShapeDtypeStruct((width, width), F32),
            jax.ShapeDtypeStruct((width, width), F32),
        ],
        compiler_params=params(),
        cost_estimate=cost(peers * rows * width, 2 * peers * rows * width + 6 * blocks * block * width),
        name="last_sum",
    )(cols, got, base)


def exchange(x):
    return lax.all_to_all(x, AXES, split_axis=0, concat_axis=0, tiled=True)


def body(
    grad_out,
    preact,
    features,
    neighbour_mean,
    w_self,
    w_neigh,
    degrees,
    tile_values,
    tile_list,
    send_counts,
):
    nodes, width = grad_out.shape
    block = tile_values.shape[1]
    peers = lax.axis_size("gx") * lax.axis_size("gy")
    capacity = tile_values.shape[0] // peers
    scale = 1.0 / math.sqrt(nodes * peers)
    slot_list = tile_list[0]
    counts = send_counts[0]
    tiles = tile_values.reshape(peers, capacity, block, block)
    last = capacity - 1

    grad_neighbour, st, gw = node_stage(
        grad_out, preact, features, neighbour_mean, w_neigh, degrees, block, scale
    )
    sent1 = terms(slot_list, counts, st, tiles, (last,), True, gw)
    got1 = exchange(sent1)
    sent2 = terms(slot_list, counts, st, tiles, tuple(range(last)), False)

    extra = got1[:, block : block + EXTRA, :]
    share = jnp.sum(extra[:, :4, :].astype(F32), axis=0)
    share = share[:2] + share[2:]
    high = share.astype(BF16)
    low = (share - high.astype(F32)).astype(BF16)
    pay = jnp.concatenate([high, low, jnp.zeros((EXTRA - 4, width), BF16)], axis=0)
    sent2 = lax.dynamic_update_slice(
        sent2, jnp.broadcast_to(pay[None], (peers, EXTRA, width)), (0, last * block, 0)
    )
    got2 = exchange(sent2)
    cols = extra[:, 4, :8].astype(jnp.int32).T
    base = first_sum(cols, got1, grad_out, preact, w_self)
    grad_features, grad_w_self, grad_w_neigh = last_sum(cols, got2, base, last)
    return (grad_features.reshape(nodes, width), grad_neighbour, grad_w_self, grad_w_neigh)


def solution(mesh):
    placed = (
        P(AXES, None),
        P(AXES, None),
        P(AXES, None),
        P(AXES, None),
        P(),
        P(),
        P(AXES),
        P(AXES, None, None),
        P(AXES, None, None),
        P(AXES, None),
    )
    return jax.shard_map(
        body,
        mesh=mesh,
        in_specs=placed,
        out_specs=(P(AXES, None), P(AXES, None), P(), P()),
        check_vma=False,
    )
```

```python
import functools
import math

import jax
import jax.numpy as jnp
from jax import lax
from jax.experimental import pallas as pl
from jax.experimental.pallas import tpu as pltpu
from jax.sharding import PartitionSpec as P

BF16 = jnp.bfloat16
F32 = jnp.float32
AXES = ("gx", "gy")
NT = (((1,), (1,)), ((), ()))
TN = (((0,), (0,)), ((), ()))
VMEM_LIMIT = 50 * 1024 * 1024
FULL_VMEM = 60 * 1024 * 1024
EXTRA = 8


def dot(a, b, dims=(((1,), (0,)), ((), ()))):
    return lax.dot_general(a, b, dims, preferred_element_type=F32)


def params():
    return pltpu.CompilerParams(
        dimension_semantics=("arbitrary",), vmem_limit_bytes=VMEM_LIMIT
    )


def cost(flops, nbytes):
    return pl.CostEstimate(flops=flops, bytes_accessed=nbytes, transcendentals=0)


def local(index, blocks):
    return index & (blocks - 1) if blocks & (blocks - 1) == 0 else lax.rem(index, blocks)


def relu_of(grad_ref, pre_ref):
    grad = grad_ref[...]
    return jnp.where(pre_ref[...] > 0, grad, jnp.zeros_like(grad))


def scaled_rows(wn, relu_t, deg, st_ref, at):
    block = deg.shape[1]
    ngt = dot(wn, relu_t)
    inv = 1.0 / deg.astype(F32)
    for b in range(deg.shape[0]):
        st_ref[at + b] = (ngt[:, b * block : (b + 1) * block] * inv[b : b + 1, :]).astype(BF16)


def node_kernel(grad_ref, pre_ref, wn_ref, deg_ref, gn_ref, st_ref):
    relu = relu_of(grad_ref, pre_ref)
    wn = wn_ref[...]
    gn_ref[...] = dot(relu, wn, NT).astype(BF16)
    scaled_rows(wn, relu.T, deg_ref[...], st_ref, 0)


def node_stage(grad_out, preact, w_neigh, degrees):
    rows, width = grad_out.shape
    blocks, block = degrees.shape
    tile = 8 * block
    node = pl.BlockSpec((tile, width), lambda i: (i, 0))
    return pl.pallas_call(
        node_kernel,
        grid=(rows // tile,),
        in_specs=[
            node,
            node,
            pl.BlockSpec((width, width), lambda i: (0, 0)),
            pl.BlockSpec((8, block), lambda i: (i, 0)),
        ],
        out_specs=[node, pl.BlockSpec((8, width, block), lambda i: (i, 0, 0))],
        out_shape=[
            jax.ShapeDtypeStruct((rows, width), BF16),
            jax.ShapeDtypeStruct((blocks, width, block), BF16),
        ],
        compiler_params=params(),
        cost_estimate=cost(4 * rows * width * width, 8 * rows * width),
        name="node_stage",
    )(grad_out, preact, w_neigh, degrees)


def hi_lo_rows(a, b, tail):
    width = a.shape[1]
    row = lax.broadcasted_iota(jnp.int32, (EXTRA, width), 0)
    a = jnp.broadcast_to(a, (EXTRA, width))
    b = jnp.broadcast_to(b, (EXTRA, width))
    a_hi = a.astype(BF16).astype(F32)
    b_hi = b.astype(BF16).astype(F32)
    out = jnp.where(row == 0, a_hi, jnp.where(row == 1, b_hi, jnp.where(row == 2, a - a_hi, b - b_hi)))
    return jnp.where(row < 4, out, jnp.where(row == 4, tail, 0.0))


def term_rows(slots, capacity, group, step, list_ref, count_ref, st_ref, tile_ref, out_ref, at, transposed, share):
    blocks, width, _ = st_ref.shape
    base = len(slots) * width
    for d in range(group):
        dest = step * group + d
        for k, slot in enumerate(slots):
            rows_t = st_ref[local(list_ref[0, dest * capacity + slot], blocks)]
            if transposed:
                term = dot(rows_t, tile_ref[at + d, k])
            else:
                term = dot(tile_ref[at + d, k], rows_t, (((0,), (1,)), ((), ())))
            keep = slot < count_ref[0, dest]
            out_ref[at + d, k * width : (k + 1) * width, :] = jnp.where(keep, term, 0.0).astype(BF16)
        if share is None:
            extra = jnp.zeros((EXTRA, width), BF16)
        else:
            lane = lax.broadcasted_iota(jnp.int32, (1, width), 1)
            cols = jnp.zeros((1, width), jnp.int32)
            for c in range(capacity):
                cols = jnp.where(lane == c, local(list_ref[1, dest * capacity + c], blocks), cols)
            extra = hi_lo_rows(
                share[d : d + 1, :width],
                share[d : d + 1, width:],
                jnp.broadcast_to(cols.astype(F32), (EXTRA, width)),
            ).astype(BF16)
        out_ref[at + d, base : base + EXTRA, :] = extra


def term_kernel(slots, capacity, group, list_ref, count_ref, st_ref, tile_ref, out_ref):
    step = pl.program_id(0)
    term_rows(slots, capacity, group, step, list_ref, count_ref, st_ref, tile_ref, out_ref, 0, False, None)


def terms(tile_list, counts, st, tiles, slots, group=16):
    peers, capacity, block, _ = tiles.shape
    blocks, width, _ = st.shape
    n = len(slots)
    at = slots[0] // n
    rows = n * block + EXTRA
    return pl.pallas_call(
        functools.partial(term_kernel, slots, capacity, group),
        grid_spec=pltpu.PrefetchScalarGridSpec(
            num_scalar_prefetch=2,
            grid=(peers // group,),
            in_specs=[
                pl.BlockSpec((blocks, width, block), lambda i, *_: (0, 0, 0)),
                pl.BlockSpec((group, n, block, block), lambda i, *_: (i, at, 0, 0)),
            ],
            out_specs=pl.BlockSpec((group, rows, width), lambda i, *_: (i, 0, 0)),
        ),
        out_shape=jax.ShapeDtypeStruct((peers, rows, width), BF16),
        compiler_params=params(),
        cost_estimate=cost(2 * peers * n * block**3, 4 * peers * n * block * block),
        name="terms",
    )(tile_list, counts, st, tiles)


def first_kernel(
    scale, slot, chunks, groups,
    list_hbm, count_hbm, deg_hbm, wn_hbm, grad_hbm, pre_hbm, feat_hbm, mean_hbm, tile_hbm,
    out_hbm,
    list_ref, count_ref, deg_ref, wn_ref, grad_ref, pre_ref, feat_ref, mean_ref, tile_ref, out_ref, st_ref, gw_ref,
    small_sem, node_sem, tile_sem, out_sem,
):
    nodes, width = grad_ref.shape
    peers, capacity = tile_hbm.shape[:2]
    part = nodes // chunks
    group = peers // groups
    small = [
        pltpu.make_async_copy(src, dst, small_sem.at[i])
        for i, (src, dst) in enumerate(
            ((wn_hbm, wn_ref), (deg_hbm, deg_ref), (list_hbm, list_ref), (count_hbm, count_ref))
        )
    ]
    pairs = ((grad_hbm, grad_ref), (pre_hbm, pre_ref), (feat_hbm, feat_ref), (mean_hbm, mean_ref))

    def node_copies(c):
        at = pl.ds(pl.multiple_of(c * part, part), part)
        return [
            pltpu.make_async_copy(src.at[at], dst.at[at], node_sem.at[i, c])
            for i, (src, dst) in enumerate(pairs)
        ]

    def tile_copy(g):
        at = pl.ds(g * group, group)
        return pltpu.make_async_copy(tile_hbm.at[at, slot : slot + 1], tile_ref.at[at], tile_sem.at[g])

    def out_copy(g):
        at = pl.ds(g * group, group)
        return pltpu.make_async_copy(out_ref.at[at], out_hbm.at[at], out_sem.at[g])

    for copy in small[:2]:
        copy.start()
    for c in range(chunks):
        for copy in node_copies(c):
            copy.start()
    for copy in small[2:]:
        copy.start()
    for g in range(groups):
        tile_copy(g).start()
    gw_ref[...] = jnp.zeros_like(gw_ref)
    for copy in small[:2]:
        copy.wait()

    @pl.loop(0, chunks)
    def _(c):
        for copy in node_copies(c):
            copy.wait()
        at = pl.ds(pl.multiple_of(c * part, part), part)
        relu_t = relu_of(grad_ref.at[at], pre_ref.at[at]).T
        rows = part // deg_ref.shape[1]
        deg = deg_ref[pl.ds(pl.multiple_of(c * rows, rows), rows), :]
        scaled_rows(wn_ref[...], relu_t, deg, st_ref, c * rows)
        gw_ref[:, :width] += dot(relu_t, feat_ref[at, :]) * scale
        gw_ref[:, width:] += dot(relu_t, mean_ref[at, :]) * scale

    for copy in small[2:]:
        copy.wait()

    @pl.loop(0, groups)
    def _(g):
        tile_copy(g).wait()
        share = gw_ref[pl.ds(pl.multiple_of(g * group, group), group), :]
        term_rows(
            (slot,), capacity, group, g, list_ref, count_ref, st_ref,
            tile_ref, out_ref, g * group, True, share,
        )
        out_copy(g).start()

    for g in range(groups):
        out_copy(g).wait()


def first_stage(tile_list, counts, degrees, w_neigh, grad_out, preact, features, mean, tiles, slot, scale, chunks=4, groups=4):
    nodes, width = grad_out.shape
    peers, capacity, block, _ = tiles.shape
    blocks = nodes // block
    rows = block + EXTRA
    hbm = pl.BlockSpec(memory_space=pl.ANY)
    node = pltpu.VMEM((nodes, width), BF16)
    return pl.pallas_call(
        functools.partial(first_kernel, scale, slot, chunks, groups),
        in_specs=[hbm] * 9,
        out_specs=hbm,
        out_shape=jax.ShapeDtypeStruct((peers, rows, width), BF16),
        scratch_shapes=[
            pltpu.SMEM(tile_list.shape, jnp.int32),
            pltpu.SMEM(counts.shape, jnp.int32),
            pltpu.VMEM(degrees.shape, jnp.int32),
            pltpu.VMEM(w_neigh.shape, BF16),
            node,
            node,
            node,
            node,
            pltpu.VMEM((peers, 1, block, block), BF16),
            pltpu.VMEM((peers, rows, width), BF16),
            pltpu.VMEM((blocks, width, block), BF16),
            pltpu.VMEM((width, 2 * width), F32),
            pltpu.SemaphoreType.DMA((4,)),
            pltpu.SemaphoreType.DMA((4, chunks)),
            pltpu.SemaphoreType.DMA((groups,)),
            pltpu.SemaphoreType.DMA((groups,)),
        ],
        compiler_params=pltpu.CompilerParams(vmem_limit_bytes=FULL_VMEM),
        cost_estimate=cost(6 * nodes * width * width + 2 * peers * block**3, 8 * nodes * width + 4 * peers * block * block),
        name="first_stage",
    )(tile_list, counts, degrees, w_neigh, grad_out, preact, features, mean, tiles)


def first_sum_kernel(group, cols_ref, got_ref, grad_ref, pre_ref, ws_ref, out_ref, acc):
    step = pl.program_id(0)
    steps = pl.num_programs(0)
    block = acc.shape[1]

    @pl.when(step == 0)
    def _():
        acc[...] = jnp.zeros_like(acc)

    for d in range(group):
        col = cols_ref[2, step * group + d]
        acc[col] += got_ref[d, :block, :].astype(F32)

    @pl.when(step == steps - 1)
    def _():
        @pl.loop(0, acc.shape[0])
        def _(b):
            at = pl.ds(pl.multiple_of(b * block, block), block)
            relu = relu_of(grad_ref.at[at], pre_ref.at[at])
            out_ref[b] = acc[b].T + dot(relu, ws_ref[...], NT)


def first_sum(cols, got, grad_out, preact, w_self, group=8):
    peers, rows, width = got.shape
    nodes = grad_out.shape[0]
    block = rows - EXTRA
    blocks = nodes // block
    whole = pl.BlockSpec((nodes, width), lambda i, *_: (0, 0))
    return pl.pallas_call(
        functools.partial(first_sum_kernel, group),
        grid_spec=pltpu.PrefetchScalarGridSpec(
            num_scalar_prefetch=1,
            grid=(peers // group,),
            in_specs=[
                pl.BlockSpec((group, rows, width), lambda i, *_: (i, 0, 0)),
                whole,
                whole,
                pl.BlockSpec((width, width), lambda i, *_: (0, 0)),
            ],
            out_specs=pl.BlockSpec((blocks, block, width), lambda i, *_: (0, 0, 0)),
            scratch_shapes=[pltpu.VMEM((blocks, block, width), F32)],
        ),
        out_shape=jax.ShapeDtypeStruct((blocks, block, width), F32),
        compiler_params=params(),
        cost_estimate=cost(2 * nodes * width * width, 2 * peers * rows * width + 8 * nodes * width),
        name="first_sum",
    )(cols, got, grad_out, preact, w_self)


def last_sum_kernel(
    slots, groups, parts, cols_ref, got_hbm, base_hbm, out_hbm, gs_ref, gn_ref,
    got, out, acc, gw, got_sem, base_sem, out_sem,
):
    peers = got.shape[0]
    blocks, block, width = acc.shape[1:]
    group = peers // groups
    part = blocks // parts

    def got_copy(g):
        at = pl.ds(g * group, group)
        return pltpu.make_async_copy(got_hbm.at[at], got.at[at], got_sem.at[g])

    def out_copy(p):
        at = pl.ds(p * part, part)
        return pltpu.make_async_copy(out.at[at], out_hbm.at[at], out_sem.at[p])

    load = pltpu.make_async_copy(base_hbm, acc.at[0], base_sem)
    load.start()
    for g in range(groups):
        got_copy(g).start()

    for k in range(1, slots):
        @pl.loop(0, blocks, unroll=4)
        def _(b):
            acc[k, b] = jnp.zeros((block, width), F32)

    load.wait()

    @pl.loop(0, groups)
    def _(g):
        got_copy(g).wait()
        for d8 in range(0, group, 8):
            shares = []
            for d in range(d8, d8 + 8):
                src = g * group + d
                for k in range(slots):
                    col = cols_ref[k, src]
                    acc[k, col] += got[src, k * block : (k + 1) * block, :].astype(F32)
                extra = got[src, slots * block : slots * block + EXTRA, :].astype(F32)
                shares.append(extra[:2] + extra[2:4])
            at = pl.ds(pl.multiple_of(g * group + d8, 8), 8)
            gw[at, :width] = jnp.concatenate([share[:1] for share in shares], axis=0)
            gw[at, width:] = jnp.concatenate([share[1:] for share in shares], axis=0)

    @pl.loop(0, parts)
    def _(p):
        for b in range(part):
            total = acc[0, p * part + b]
            for k in range(1, slots):
                total += acc[k, p * part + b]
            out[p * part + b] = total.astype(BF16)
        out_copy(p).start()

    gs_ref[...] = gw[:, :width].T
    gn_ref[...] = gw[:, width:].T
    for p in range(parts):
        out_copy(p).wait()


def last_sum(cols, got, base, slots, groups=4, parts=4):
    peers, rows, width = got.shape
    blocks, block, _ = base.shape
    hbm = pl.BlockSpec(memory_space=pl.ANY)
    vmem = pl.BlockSpec(memory_space=pltpu.VMEM)
    return pl.pallas_call(
        functools.partial(last_sum_kernel, slots, groups, parts),
        in_specs=[pl.BlockSpec(memory_space=pltpu.SMEM), hbm, hbm],
        out_specs=[hbm, vmem, vmem],
        scratch_shapes=[
            pltpu.VMEM((peers, rows, width), BF16),
            pltpu.VMEM((blocks, block, width), BF16),
            pltpu.VMEM((slots, blocks, block, width), F32),
            pltpu.VMEM((width, 2 * width), F32),
            pltpu.SemaphoreType.DMA((groups,)),
            pltpu.SemaphoreType.DMA,
            pltpu.SemaphoreType.DMA((parts,)),
        ],
        out_shape=[
            jax.ShapeDtypeStruct((blocks, block, width), BF16),
            jax.ShapeDtypeStruct((width, width), F32),
            jax.ShapeDtypeStruct((width, width), F32),
        ],
        compiler_params=pltpu.CompilerParams(vmem_limit_bytes=FULL_VMEM),
        cost_estimate=cost(peers * rows * width, 2 * peers * rows * width + 6 * blocks * block * width),
        name="last_sum",
    )(cols, got, base)


def exchange(x):
    return lax.all_to_all(x, AXES, split_axis=0, concat_axis=0, tiled=True)


def body(
    grad_out,
    preact,
    features,
    neighbour_mean,
    w_self,
    w_neigh,
    degrees,
    tile_values,
    tile_list,
    send_counts,
):
    nodes, width = grad_out.shape
    block = tile_values.shape[1]
    peers = lax.axis_size("gx") * lax.axis_size("gy")
    capacity = tile_values.shape[0] // peers
    scale = 1.0 / math.sqrt(nodes * peers)
    slot_list = tile_list[0]
    tiles = tile_values.reshape(peers, capacity, block, block)
    last = capacity - 1

    degrees = degrees.reshape(nodes // block, block)
    sent1 = first_stage(
        slot_list, send_counts, degrees, w_neigh, grad_out, preact, features, neighbour_mean,
        tiles, last, scale,
    )
    got1 = exchange(sent1)
    grad_neighbour, st = node_stage(grad_out, preact, w_neigh, degrees)
    sent2 = terms(slot_list, send_counts, st, tiles, tuple(range(last)))

    extra = got1[:, block : block + EXTRA, :]
    share = jnp.sum(extra[:, :4, :].astype(F32), axis=0)
    share = share[:2] + share[2:]
    high = lax.reduce_precision(share, exponent_bits=8, mantissa_bits=7)
    low = share - high
    pay = jnp.concatenate([high, low, jnp.zeros((EXTRA - 4, width), F32)], axis=0).astype(BF16)
    sent2 = lax.dynamic_update_slice(
        sent2, jnp.broadcast_to(pay[None], (peers, EXTRA, width)), (0, last * block, 0)
    )
    got2 = exchange(sent2)
    cols = extra[:, 4, :8].astype(jnp.int32).T
    base = first_sum(cols, got1, grad_out, preact, w_self)
    grad_features, grad_w_self, grad_w_neigh = last_sum(cols, got2, base, last)
    return (grad_features.reshape(nodes, width), grad_neighbour, grad_w_self, grad_w_neigh)


def solution(mesh):
    placed = (
        P(AXES, None),
        P(AXES, None),
        P(AXES, None),
        P(AXES, None),
        P(),
        P(),
        P(AXES),
        P(AXES, None, None),
        P(AXES, None, None),
        P(AXES, None),
    )
    return jax.shard_map(
        body,
        mesh=mesh,
        in_specs=placed,
        out_specs=(P(AXES, None), P(AXES, None), P(), P()),
        check_vma=False,
    )
```

```python
import functools
import math

import jax
import jax.numpy as jnp
from jax import lax
from jax.experimental import pallas as pl
from jax.experimental.pallas import tpu as pltpu
from jax.sharding import PartitionSpec as P

BF16 = jnp.bfloat16
F32 = jnp.float32
CORES = 2
AXES = ("z", "core", "gy")
NT = (((1,), (1,)), ((), ()))
TN = (((0,), (0,)), ((), ()))
VMEM_LIMIT = 50 * 1024 * 1024
FULL_VMEM = 60 * 1024 * 1024
EXTRA = 8


def dot(a, b, dims=(((1,), (0,)), ((), ()))):
    return lax.dot_general(a, b, dims, preferred_element_type=F32)


def params():
    return pltpu.CompilerParams(
        dimension_semantics=("arbitrary",), vmem_limit_bytes=VMEM_LIMIT
    )


def cost(flops, nbytes):
    return pl.CostEstimate(flops=flops, bytes_accessed=nbytes, transcendentals=0)


def local(index, blocks):
    return index & (blocks - 1) if blocks & (blocks - 1) == 0 else lax.rem(index, blocks)


def order(group, cores):
    return [d % (group // cores) * cores + d // (group // cores) for d in range(group)]


def relu_of(grad_ref, pre_ref):
    grad = grad_ref[...]
    return jnp.where(pre_ref[...] > 0, grad, jnp.zeros_like(grad))


def scaled_rows(wn, relu_t, deg, st_ref, at):
    block = deg.shape[1]
    ngt = dot(wn, relu_t)
    inv = 1.0 / deg.astype(F32)
    for b in range(deg.shape[0]):
        st_ref[at + b] = (ngt[:, b * block : (b + 1) * block] * inv[b : b + 1, :]).astype(BF16)


def node_kernel(grad_ref, pre_ref, wn_ref, deg_ref, gn_ref, st_ref):
    relu = relu_of(grad_ref, pre_ref)
    wn = wn_ref[...]
    gn_ref[...] = dot(relu, wn, NT).astype(BF16)
    scaled_rows(wn, relu.T, deg_ref[...], st_ref, 0)


def node_stage(grad_out, preact, w_neigh, degrees):
    rows, width = grad_out.shape
    blocks, block = degrees.shape
    tile = 8 * block
    node = pl.BlockSpec((tile, width), lambda i: (i, 0))
    return pl.pallas_call(
        node_kernel,
        grid=(rows // tile,),
        in_specs=[
            node,
            node,
            pl.BlockSpec((width, width), lambda i: (0, 0)),
            pl.BlockSpec((8, block), lambda i: (i, 0)),
        ],
        out_specs=[node, pl.BlockSpec((8, width, block), lambda i: (i, 0, 0))],
        out_shape=[
            jax.ShapeDtypeStruct((rows, width), BF16),
            jax.ShapeDtypeStruct((blocks, width, block), BF16),
        ],
        compiler_params=params(),
        cost_estimate=cost(4 * rows * width * width, 8 * rows * width),
        name="node_stage",
    )(grad_out, preact, w_neigh, degrees)


def hi_lo_rows(a, b, tail):
    width = a.shape[1]
    row = lax.broadcasted_iota(jnp.int32, (EXTRA, width), 0)
    a = jnp.broadcast_to(a, (EXTRA, width))
    b = jnp.broadcast_to(b, (EXTRA, width))
    a_hi = a.astype(BF16).astype(F32)
    b_hi = b.astype(BF16).astype(F32)
    out = jnp.where(row == 0, a_hi, jnp.where(row == 1, b_hi, jnp.where(row == 2, a - a_hi, b - b_hi)))
    return jnp.where(row < 4, out, jnp.where(row == 4, tail, 0.0))


def term_rows(slots, capacity, places, step, list_ref, count_ref, st_ref, tile_ref, out_ref, at, transposed, share):
    blocks, width, _ = st_ref.shape
    base = len(slots) * width
    for d, place in enumerate(places):
        dest = step * len(places) + d
        for k, slot in enumerate(slots):
            rows_t = st_ref[local(list_ref[0, dest * capacity + slot], blocks)]
            if transposed:
                term = dot(rows_t, tile_ref[at + d, k])
            else:
                term = dot(tile_ref[at + d, k], rows_t, (((0,), (1,)), ((), ())))
            keep = slot < count_ref[0, dest]
            out_ref[at + place, k * width : (k + 1) * width, :] = jnp.where(keep, term, 0.0).astype(BF16)
        if share is None:
            extra = jnp.zeros((EXTRA, width), BF16)
        else:
            lane = lax.broadcasted_iota(jnp.int32, (1, width), 1)
            cols = jnp.zeros((1, width), jnp.int32)
            for c in range(capacity):
                cols = jnp.where(lane == c, local(list_ref[1, dest * capacity + c], blocks), cols)
            extra = hi_lo_rows(
                share[d : d + 1, :width],
                share[d : d + 1, width:],
                jnp.broadcast_to(cols.astype(F32), (EXTRA, width)),
            ).astype(BF16)
        out_ref[at + place, base : base + EXTRA, :] = extra


def term_kernel(slots, capacity, places, list_ref, count_ref, st_ref, tile_ref, out_ref):
    step = pl.program_id(0)
    term_rows(slots, capacity, places, step, list_ref, count_ref, st_ref, tile_ref, out_ref, 0, False, None)


def terms(tile_list, counts, st, tiles, slots, places):
    peers, capacity, block, _ = tiles.shape
    blocks, width, _ = st.shape
    n = len(slots)
    at = slots[0] // n
    group = len(places)
    rows = n * block + EXTRA
    return pl.pallas_call(
        functools.partial(term_kernel, slots, capacity, places),
        grid_spec=pltpu.PrefetchScalarGridSpec(
            num_scalar_prefetch=2,
            grid=(peers // group,),
            in_specs=[
                pl.BlockSpec((blocks, width, block), lambda i, *_: (0, 0, 0)),
                pl.BlockSpec((group, n, block, block), lambda i, *_: (i, at, 0, 0)),
            ],
            out_specs=pl.BlockSpec((group, rows, width), lambda i, *_: (i, 0, 0)),
        ),
        out_shape=jax.ShapeDtypeStruct((peers, rows, width), BF16),
        compiler_params=params(),
        cost_estimate=cost(2 * peers * n * block**3, 4 * peers * n * block * block),
        name="terms",
    )(tile_list, counts, st, tiles)


def first_kernel(
    scale, slot, chunks, places,
    list_hbm, count_hbm, deg_hbm, wn_hbm, grad_hbm, pre_hbm, feat_hbm, mean_hbm, tile_hbm,
    out_hbm,
    list_ref, count_ref, deg_ref, wn_ref, grad_ref, pre_ref, feat_ref, mean_ref, tile_ref, out_ref, st_ref, gw_ref,
    small_sem, node_sem, tile_sem, out_sem,
):
    nodes, width = grad_ref.shape
    peers, capacity = tile_hbm.shape[:2]
    part = nodes // chunks
    group = len(places)
    groups = peers // group
    small = [
        pltpu.make_async_copy(src, dst, small_sem.at[i])
        for i, (src, dst) in enumerate(
            ((wn_hbm, wn_ref), (deg_hbm, deg_ref), (list_hbm, list_ref), (count_hbm, count_ref))
        )
    ]
    pairs = ((grad_hbm, grad_ref), (pre_hbm, pre_ref), (feat_hbm, feat_ref), (mean_hbm, mean_ref))

    def node_copies(c):
        at = pl.ds(pl.multiple_of(c * part, part), part)
        return [
            pltpu.make_async_copy(src.at[at], dst.at[at], node_sem.at[i, c])
            for i, (src, dst) in enumerate(pairs)
        ]

    def tile_copy(g):
        at = pl.ds(g * group, group)
        return pltpu.make_async_copy(tile_hbm.at[at, slot : slot + 1], tile_ref.at[at], tile_sem.at[g])

    def out_copy(g):
        at = pl.ds(g * group, group)
        return pltpu.make_async_copy(out_ref.at[at], out_hbm.at[at], out_sem.at[g])

    for copy in small[:2]:
        copy.start()
    for c in range(chunks):
        for copy in node_copies(c):
            copy.start()
    for copy in small[2:]:
        copy.start()
    for g in range(groups):
        tile_copy(g).start()
    gw_ref[...] = jnp.zeros_like(gw_ref)
    for copy in small[:2]:
        copy.wait()

    @pl.loop(0, chunks)
    def _(c):
        for copy in node_copies(c):
            copy.wait()
        at = pl.ds(pl.multiple_of(c * part, part), part)
        relu_t = relu_of(grad_ref.at[at], pre_ref.at[at]).T
        rows = part // deg_ref.shape[1]
        deg = deg_ref[pl.ds(pl.multiple_of(c * rows, rows), rows), :]
        scaled_rows(wn_ref[...], relu_t, deg, st_ref, c * rows)
        gw_ref[:, :width] += dot(relu_t, feat_ref[at, :]) * scale
        gw_ref[:, width:] += dot(relu_t, mean_ref[at, :]) * scale

    for copy in small[2:]:
        copy.wait()

    @pl.loop(0, groups)
    def _(g):
        tile_copy(g).wait()
        share = gw_ref[pl.ds(pl.multiple_of(g * group, group), group), :]
        term_rows(
            (slot,), capacity, places, g, list_ref, count_ref, st_ref,
            tile_ref, out_ref, g * group, True, share,
        )
        out_copy(g).start()

    for g in range(groups):
        out_copy(g).wait()


def first_stage(tile_list, counts, degrees, w_neigh, grad_out, preact, features, mean, tiles, slot, scale, places, chunks=2):
    nodes, width = grad_out.shape
    peers, capacity, block, _ = tiles.shape
    blocks = nodes // block
    rows = block + EXTRA
    groups = peers // len(places)
    hbm = pl.BlockSpec(memory_space=pl.ANY)
    node = pltpu.VMEM((nodes, width), BF16)
    return pl.pallas_call(
        functools.partial(first_kernel, scale, slot, chunks, places),
        in_specs=[hbm] * 9,
        out_specs=hbm,
        out_shape=jax.ShapeDtypeStruct((peers, rows, width), BF16),
        scratch_shapes=[
            pltpu.SMEM(tile_list.shape, jnp.int32),
            pltpu.SMEM(counts.shape, jnp.int32),
            pltpu.VMEM(degrees.shape, jnp.int32),
            pltpu.VMEM(w_neigh.shape, BF16),
            node,
            node,
            node,
            node,
            pltpu.VMEM((peers, 1, block, block), BF16),
            pltpu.VMEM((peers, rows, width), BF16),
            pltpu.VMEM((blocks, width, block), BF16),
            pltpu.VMEM((width, 2 * width), F32),
            pltpu.SemaphoreType.DMA((4,)),
            pltpu.SemaphoreType.DMA((4, chunks)),
            pltpu.SemaphoreType.DMA((groups,)),
            pltpu.SemaphoreType.DMA((groups,)),
        ],
        compiler_params=pltpu.CompilerParams(vmem_limit_bytes=FULL_VMEM),
        cost_estimate=cost(6 * nodes * width * width + 2 * peers * block**3, 8 * nodes * width + 4 * peers * block * block),
        name="first_stage",
    )(tile_list, counts, degrees, w_neigh, grad_out, preact, features, mean, tiles)


def first_sum_kernel(group, cols_ref, got_ref, grad_ref, pre_ref, ws_ref, out_ref, acc):
    step = pl.program_id(0)
    steps = pl.num_programs(0)
    block = acc.shape[1]

    @pl.when(step == 0)
    def _():
        acc[...] = jnp.zeros_like(acc)

    for d in range(group):
        col = cols_ref[2, step * group + d]
        acc[col] += got_ref[d, :block, :].astype(F32)

    @pl.when(step == steps - 1)
    def _():
        @pl.loop(0, acc.shape[0])
        def _(b):
            at = pl.ds(pl.multiple_of(b * block, block), block)
            relu = relu_of(grad_ref.at[at], pre_ref.at[at])
            out_ref[b] = acc[b].T + dot(relu, ws_ref[...], NT)


def first_sum(cols, got, grad_out, preact, w_self, group=8):
    peers, rows, width = got.shape
    nodes = grad_out.shape[0]
    block = rows - EXTRA
    blocks = nodes // block
    whole = pl.BlockSpec((nodes, width), lambda i, *_: (0, 0))
    return pl.pallas_call(
        functools.partial(first_sum_kernel, group),
        grid_spec=pltpu.PrefetchScalarGridSpec(
            num_scalar_prefetch=1,
            grid=(peers // group,),
            in_specs=[
                pl.BlockSpec((group, rows, width), lambda i, *_: (i, 0, 0)),
                whole,
                whole,
                pl.BlockSpec((width, width), lambda i, *_: (0, 0)),
            ],
            out_specs=pl.BlockSpec((blocks, block, width), lambda i, *_: (0, 0, 0)),
            scratch_shapes=[pltpu.VMEM((blocks, block, width), F32)],
        ),
        out_shape=jax.ShapeDtypeStruct((blocks, block, width), F32),
        compiler_params=params(),
        cost_estimate=cost(2 * nodes * width * width, 2 * peers * rows * width + 8 * nodes * width),
        name="first_sum",
    )(cols, got, grad_out, preact, w_self)


def last_sum_kernel(
    slots, places, parts, cols_ref, got_hbm, base_hbm, out_hbm, gs_ref, gn_ref,
    got, out, acc, gw, got_sem, base_sem, out_sem,
):
    peers = got.shape[0]
    blocks, block, width = acc.shape[1:]
    group = len(places)
    groups = peers // group
    part = blocks // parts

    def got_copy(g):
        at = pl.ds(g * group, group)
        return pltpu.make_async_copy(got_hbm.at[at], got.at[at], got_sem.at[g])

    def out_copy(p):
        at = pl.ds(p * part, part)
        return pltpu.make_async_copy(out.at[at], out_hbm.at[at], out_sem.at[p])

    load = pltpu.make_async_copy(base_hbm, acc.at[0], base_sem)
    load.start()
    for g in range(groups):
        got_copy(g).start()

    for k in range(1, slots):
        @pl.loop(0, blocks, unroll=4)
        def _(b):
            acc[k, b] = jnp.zeros((block, width), F32)

    load.wait()

    @pl.loop(0, groups)
    def _(g):
        got_copy(g).wait()
        shares = []
        for d in range(group):
            src = g * group + d
            for k in range(slots):
                col = cols_ref[k, src]
                acc[k, col] += got[src, k * block : (k + 1) * block, :].astype(F32)
            extra = got[src, slots * block : slots * block + EXTRA, :].astype(F32)
            shares.append(extra[:2] + extra[2:4])
        shares = [shares[place] for place in places]
        at = pl.ds(pl.multiple_of(g * group, group), group)
        gw[at, :width] = jnp.concatenate([share[:1] for share in shares], axis=0)
        gw[at, width:] = jnp.concatenate([share[1:] for share in shares], axis=0)

    @pl.loop(0, parts)
    def _(p):
        for b in range(part):
            total = acc[0, p * part + b]
            for k in range(1, slots):
                total += acc[k, p * part + b]
            out[p * part + b] = total.astype(BF16)
        out_copy(p).start()

    gs_ref[...] = gw[:, :width].T
    gn_ref[...] = gw[:, width:].T
    for p in range(parts):
        out_copy(p).wait()


def last_sum(cols, got, base, slots, places, parts=4):
    peers, rows, width = got.shape
    blocks, block, _ = base.shape
    groups = peers // len(places)
    hbm = pl.BlockSpec(memory_space=pl.ANY)
    vmem = pl.BlockSpec(memory_space=pltpu.VMEM)
    return pl.pallas_call(
        functools.partial(last_sum_kernel, slots, places, parts),
        in_specs=[pl.BlockSpec(memory_space=pltpu.SMEM), hbm, hbm],
        out_specs=[hbm, vmem, vmem],
        scratch_shapes=[
            pltpu.VMEM((peers, rows, width), BF16),
            pltpu.VMEM((blocks, block, width), BF16),
            pltpu.VMEM((slots, blocks, block, width), F32),
            pltpu.VMEM((width, 2 * width), F32),
            pltpu.SemaphoreType.DMA((groups,)),
            pltpu.SemaphoreType.DMA,
            pltpu.SemaphoreType.DMA((parts,)),
        ],
        out_shape=[
            jax.ShapeDtypeStruct((blocks, block, width), BF16),
            jax.ShapeDtypeStruct((width, width), F32),
            jax.ShapeDtypeStruct((width, width), F32),
        ],
        compiler_params=pltpu.CompilerParams(vmem_limit_bytes=FULL_VMEM),
        cost_estimate=cost(peers * rows * width, 2 * peers * rows * width + 6 * blocks * block * width),
        name="last_sum",
    )(cols, got, base)


def exchange(x):
    return lax.all_to_all(x, ("z", "gy", "core"), split_axis=0, concat_axis=0, tiled=True)


def body(
    grad_out,
    preact,
    features,
    neighbour_mean,
    w_self,
    w_neigh,
    degrees,
    tile_values,
    tile_list,
    send_counts,
):
    nodes, width = grad_out.shape
    block = tile_values.shape[1]
    cores = lax.axis_size("core")
    group = cores * lax.axis_size("gy")
    peers = lax.axis_size("z") * group
    places = order(group, cores)
    capacity = tile_values.shape[0] // peers
    scale = 1.0 / math.sqrt(nodes * peers)
    slot_list = tile_list[0]
    tiles = tile_values.reshape(peers, capacity, block, block)
    last = capacity - 1

    degrees = degrees.reshape(nodes // block, block)
    sent1 = first_stage(
        slot_list, send_counts, degrees, w_neigh, grad_out, preact, features, neighbour_mean,
        tiles, last, scale, places,
    )
    got1 = exchange(sent1)
    grad_neighbour, st = node_stage(grad_out, preact, w_neigh, degrees)
    sent2 = terms(slot_list, send_counts, st, tiles, tuple(range(last)), places)

    extra = got1[:, block : block + EXTRA, :]
    share = jnp.sum(extra[:, :4, :].astype(F32), axis=0)
    share = share[:2] + share[2:]
    high = lax.reduce_precision(share, exponent_bits=8, mantissa_bits=7)
    low = share - high
    pay = jnp.concatenate([high, low, jnp.zeros((EXTRA - 4, width), F32)], axis=0).astype(BF16)
    sent2 = lax.dynamic_update_slice(
        sent2, jnp.broadcast_to(pay[None], (peers, EXTRA, width)), (0, last * block, 0)
    )
    got2 = exchange(sent2)
    cols = extra[:, 4, :8].astype(jnp.int32).T
    base = first_sum(cols, got1, grad_out, preact, w_self)
    grad_features, grad_w_self, grad_w_neigh = last_sum(cols, got2, base, last, places)
    return (grad_features.reshape(nodes, width), grad_neighbour, grad_w_self, grad_w_neigh)


def solution(mesh):
    major, minor = mesh.devices.shape
    mesh = jax.sharding.Mesh(mesh.devices.reshape(major // CORES, CORES, minor), AXES)
    placed = (
        P(AXES, None),
        P(AXES, None),
        P(AXES, None),
        P(AXES, None),
        P(),
        P(),
        P(AXES),
        P(AXES, None, None),
        P(AXES, None, None),
        P(AXES, None),
    )
    return jax.shard_map(
        body,
        mesh=mesh,
        in_specs=placed,
        out_specs=(P(AXES, None), P(AXES, None), P(), P()),
        check_vma=False,
    )
```

```python
import functools
import math

import jax
import jax.numpy as jnp
from jax import lax
from jax.experimental import pallas as pl
from jax.experimental.pallas import tpu as pltpu
from jax.sharding import PartitionSpec as P

BF16 = jnp.bfloat16
F32 = jnp.float32
CORES = 2
AXES = ("z", "core", "gy")
NT = (((1,), (1,)), ((), ()))
TN = (((0,), (0,)), ((), ()))
VMEM_LIMIT = 50 * 1024 * 1024
FULL_VMEM = 60 * 1024 * 1024
EXTRA = 8


def dot(a, b, dims=(((1,), (0,)), ((), ()))):
    return lax.dot_general(a, b, dims, preferred_element_type=F32)


def params():
    return pltpu.CompilerParams(
        dimension_semantics=("arbitrary",), vmem_limit_bytes=VMEM_LIMIT
    )


def cost(flops, nbytes):
    return pl.CostEstimate(flops=flops, bytes_accessed=nbytes, transcendentals=0)


def local(index, blocks):
    return index & (blocks - 1) if blocks & (blocks - 1) == 0 else lax.rem(index, blocks)


def order(group, cores):
    return [d % (group // cores) * cores + d // (group // cores) for d in range(group)]


def relu_of(grad_ref, pre_ref):
    grad = grad_ref[...]
    return jnp.where(pre_ref[...] > 0, grad, jnp.zeros_like(grad))


def scaled_rows(wn, relu_t, deg, st_ref, at):
    block = deg.shape[1]
    ngt = dot(wn, relu_t)
    inv = 1.0 / deg.astype(F32)
    for b in range(deg.shape[0]):
        st_ref[at + b] = (ngt[:, b * block : (b + 1) * block] * inv[b : b + 1, :]).astype(BF16)


def node_kernel(grad_ref, pre_ref, wn_ref, deg_ref, gn_ref, st_ref):
    relu = relu_of(grad_ref, pre_ref)
    wn = wn_ref[...]
    gn_ref[...] = dot(relu, wn, NT).astype(BF16)
    scaled_rows(wn, relu.T, deg_ref[...], st_ref, 0)


def node_stage(grad_out, preact, w_neigh, degrees):
    rows, width = grad_out.shape
    blocks, block = degrees.shape
    tile = 8 * block
    node = pl.BlockSpec((tile, width), lambda i: (i, 0))
    return pl.pallas_call(
        node_kernel,
        grid=(rows // tile,),
        in_specs=[
            node,
            node,
            pl.BlockSpec((width, width), lambda i: (0, 0)),
            pl.BlockSpec((8, block), lambda i: (i, 0)),
        ],
        out_specs=[node, pl.BlockSpec((8, width, block), lambda i: (i, 0, 0))],
        out_shape=[
            jax.ShapeDtypeStruct((rows, width), BF16),
            jax.ShapeDtypeStruct((blocks, width, block), BF16),
        ],
        compiler_params=params(),
        cost_estimate=cost(4 * rows * width * width, 8 * rows * width),
        name="node_stage",
    )(grad_out, preact, w_neigh, degrees)


def hi_lo_rows(a, b, tail):
    width = a.shape[1]
    row = lax.broadcasted_iota(jnp.int32, (EXTRA, width), 0)
    a = jnp.broadcast_to(a, (EXTRA, width))
    b = jnp.broadcast_to(b, (EXTRA, width))
    a_hi = a.astype(BF16).astype(F32)
    b_hi = b.astype(BF16).astype(F32)
    out = jnp.where(row == 0, a_hi, jnp.where(row == 1, b_hi, jnp.where(row == 2, a - a_hi, b - b_hi)))
    return jnp.where(row < 4, out, jnp.where(row == 4, tail, 0.0))


def term_rows(slots, capacity, places, step, list_ref, count_ref, st_ref, tile_ref, out_ref, at, transposed, share):
    blocks, width, _ = st_ref.shape
    base = len(slots) * width
    for d, place in enumerate(places):
        dest = step * len(places) + d
        for k, slot in enumerate(slots):
            rows_t = st_ref[local(list_ref[0, dest * capacity + slot], blocks)]
            if transposed:
                term = dot(rows_t, tile_ref[at + d, k])
            else:
                term = dot(tile_ref[at + d, k], rows_t, (((0,), (1,)), ((), ())))
            keep = slot < count_ref[0, dest]
            out_ref[at + place, k * width : (k + 1) * width, :] = jnp.where(keep, term, 0.0).astype(BF16)
        if share is None:
            extra = jnp.zeros((EXTRA, width), BF16)
        else:
            lane = lax.broadcasted_iota(jnp.int32, (1, width), 1)
            cols = jnp.zeros((1, width), jnp.int32)
            for c in range(capacity):
                cols = jnp.where(lane == c, local(list_ref[1, dest * capacity + c], blocks), cols)
            extra = hi_lo_rows(
                share[d : d + 1, :width],
                share[d : d + 1, width:],
                jnp.broadcast_to(cols.astype(F32), (EXTRA, width)),
            ).astype(BF16)
        out_ref[at + place, base : base + EXTRA, :] = extra


def term_kernel(slots, capacity, places, list_ref, count_ref, st_ref, tile_ref, out_ref):
    step = pl.program_id(0)
    term_rows(slots, capacity, places, step, list_ref, count_ref, st_ref, tile_ref, out_ref, 0, False, None)


def terms(tile_list, counts, st, tiles, slots, places):
    peers, capacity, block, _ = tiles.shape
    blocks, width, _ = st.shape
    n = len(slots)
    at = slots[0] // n
    group = len(places)
    rows = n * block + EXTRA
    return pl.pallas_call(
        functools.partial(term_kernel, slots, capacity, places),
        grid_spec=pltpu.PrefetchScalarGridSpec(
            num_scalar_prefetch=2,
            grid=(peers // group,),
            in_specs=[
                pl.BlockSpec((blocks, width, block), lambda i, *_: (0, 0, 0)),
                pl.BlockSpec((group, n, block, block), lambda i, *_: (i, at, 0, 0)),
            ],
            out_specs=pl.BlockSpec((group, rows, width), lambda i, *_: (i, 0, 0)),
        ),
        out_shape=jax.ShapeDtypeStruct((peers, rows, width), BF16),
        compiler_params=params(),
        cost_estimate=cost(2 * peers * n * block**3, 4 * peers * n * block * block),
        name="terms",
    )(tile_list, counts, st, tiles)


def first_kernel(
    scale, slot, chunks, places,
    list_hbm, count_hbm, deg_hbm, wn_hbm, grad_hbm, pre_hbm, feat_hbm, mean_hbm, tile_hbm,
    out_hbm,
    list_ref, count_ref, deg_ref, wn_ref, grad_ref, pre_ref, feat_ref, mean_ref, tile_ref, out_ref, st_ref, gw_ref,
    small_sem, node_sem, tile_sem, out_sem,
):
    nodes, width = grad_ref.shape
    peers, capacity = tile_hbm.shape[:2]
    part = nodes // chunks
    group = len(places)
    groups = peers // group
    small = [
        pltpu.make_async_copy(src, dst, small_sem.at[i])
        for i, (src, dst) in enumerate(
            ((wn_hbm, wn_ref), (deg_hbm, deg_ref), (list_hbm, list_ref), (count_hbm, count_ref))
        )
    ]
    pairs = ((grad_hbm, grad_ref), (pre_hbm, pre_ref), (feat_hbm, feat_ref), (mean_hbm, mean_ref))

    def node_copies(c):
        at = pl.ds(pl.multiple_of(c * part, part), part)
        return [
            pltpu.make_async_copy(src.at[at], dst.at[at], node_sem.at[i, c])
            for i, (src, dst) in enumerate(pairs)
        ]

    def tile_copy(g):
        at = pl.ds(g * group, group)
        return pltpu.make_async_copy(tile_hbm.at[at, slot : slot + 1], tile_ref.at[at], tile_sem.at[g])

    def out_copy(g):
        at = pl.ds(g * group, group)
        return pltpu.make_async_copy(out_ref.at[at], out_hbm.at[at], out_sem.at[g])

    for copy in small[:2]:
        copy.start()
    for c in range(chunks):
        for copy in node_copies(c):
            copy.start()
    for copy in small[2:]:
        copy.start()
    for g in range(groups):
        tile_copy(g).start()
    gw_ref[...] = jnp.zeros_like(gw_ref)
    for copy in small[:2]:
        copy.wait()

    @pl.loop(0, chunks)
    def _(c):
        for copy in node_copies(c):
            copy.wait()
        at = pl.ds(pl.multiple_of(c * part, part), part)
        relu_t = relu_of(grad_ref.at[at], pre_ref.at[at]).T
        rows = part // deg_ref.shape[1]
        deg = deg_ref[pl.ds(pl.multiple_of(c * rows, rows), rows), :]
        scaled_rows(wn_ref[...], relu_t, deg, st_ref, c * rows)
        gw_ref[:, :width] += dot(relu_t, feat_ref[at, :]) * scale
        gw_ref[:, width:] += dot(relu_t, mean_ref[at, :]) * scale

    for copy in small[2:]:
        copy.wait()

    @pl.loop(0, groups)
    def _(g):
        tile_copy(g).wait()
        share = gw_ref[pl.ds(pl.multiple_of(g * group, group), group), :]
        term_rows(
            (slot,), capacity, places, g, list_ref, count_ref, st_ref,
            tile_ref, out_ref, g * group, True, share,
        )
        out_copy(g).start()

    for g in range(groups):
        out_copy(g).wait()


def first_stage(tile_list, counts, degrees, w_neigh, grad_out, preact, features, mean, tiles, slot, scale, places, chunks=2):
    nodes, width = grad_out.shape
    peers, capacity, block, _ = tiles.shape
    blocks = nodes // block
    rows = block + EXTRA
    groups = peers // len(places)
    hbm = pl.BlockSpec(memory_space=pl.ANY)
    node = pltpu.VMEM((nodes, width), BF16)
    return pl.pallas_call(
        functools.partial(first_kernel, scale, slot, chunks, places),
        in_specs=[hbm] * 9,
        out_specs=hbm,
        out_shape=jax.ShapeDtypeStruct((peers, rows, width), BF16),
        scratch_shapes=[
            pltpu.SMEM(tile_list.shape, jnp.int32),
            pltpu.SMEM(counts.shape, jnp.int32),
            pltpu.VMEM(degrees.shape, jnp.int32),
            pltpu.VMEM(w_neigh.shape, BF16),
            node,
            node,
            node,
            node,
            pltpu.VMEM((peers, 1, block, block), BF16),
            pltpu.VMEM((peers, rows, width), BF16),
            pltpu.VMEM((blocks, width, block), BF16),
            pltpu.VMEM((width, 2 * width), F32),
            pltpu.SemaphoreType.DMA((4,)),
            pltpu.SemaphoreType.DMA((4, chunks)),
            pltpu.SemaphoreType.DMA((groups,)),
            pltpu.SemaphoreType.DMA((groups,)),
        ],
        compiler_params=pltpu.CompilerParams(vmem_limit_bytes=FULL_VMEM),
        cost_estimate=cost(6 * nodes * width * width + 2 * peers * block**3, 8 * nodes * width + 4 * peers * block * block),
        name="first_stage",
    )(tile_list, counts, degrees, w_neigh, grad_out, preact, features, mean, tiles)


def first_sum_kernel(group, cols_ref, got_ref, grad_ref, pre_ref, ws_ref, out_ref, acc):
    step = pl.program_id(0)
    steps = pl.num_programs(0)
    block = acc.shape[1]

    @pl.when(step == 0)
    def _():
        acc[...] = jnp.zeros_like(acc)

    for d in range(group):
        col = cols_ref[2, step * group + d]
        acc[col] += got_ref[d, :block, :].astype(F32)

    @pl.when(step == steps - 1)
    def _():
        @pl.loop(0, acc.shape[0])
        def _(b):
            at = pl.ds(pl.multiple_of(b * block, block), block)
            relu = relu_of(grad_ref.at[at], pre_ref.at[at])
            out_ref[b] = acc[b].T + dot(relu, ws_ref[...], NT)


def first_sum(cols, got, grad_out, preact, w_self, group=8):
    peers, rows, width = got.shape
    nodes = grad_out.shape[0]
    block = rows - EXTRA
    blocks = nodes // block
    whole = pl.BlockSpec((nodes, width), lambda i, *_: (0, 0))
    return pl.pallas_call(
        functools.partial(first_sum_kernel, group),
        grid_spec=pltpu.PrefetchScalarGridSpec(
            num_scalar_prefetch=1,
            grid=(peers // group,),
            in_specs=[
                pl.BlockSpec((group, rows, width), lambda i, *_: (i, 0, 0)),
                whole,
                whole,
                pl.BlockSpec((width, width), lambda i, *_: (0, 0)),
            ],
            out_specs=pl.BlockSpec((blocks, block, width), lambda i, *_: (0, 0, 0)),
            scratch_shapes=[pltpu.VMEM((blocks, block, width), F32)],
        ),
        out_shape=jax.ShapeDtypeStruct((blocks, block, width), F32),
        compiler_params=params(),
        cost_estimate=cost(2 * nodes * width * width, 2 * peers * rows * width + 8 * nodes * width),
        name="first_sum",
    )(cols, got, grad_out, preact, w_self)


def last_sum_kernel(
    slots, places, parts, cols_ref, got_hbm, base_hbm, out_hbm, gs_ref, gn_ref,
    got, out, base, acc, gw, got_sem, base_sem, out_sem,
):
    peers = got.shape[0]
    blocks, block, width = acc.shape
    group = len(places)
    groups = peers // group
    part = blocks // parts

    def got_copy(g):
        at = pl.ds(g * group, group)
        return pltpu.make_async_copy(got_hbm.at[at], got.at[at], got_sem.at[g])

    def out_copy(p):
        at = pl.ds(p * part, part)
        return pltpu.make_async_copy(out.at[at], out_hbm.at[at], out_sem.at[p])

    load = pltpu.make_async_copy(base_hbm, base, base_sem)
    for g in range(groups):
        got_copy(g).start()
    load.start()

    @pl.loop(0, blocks, unroll=4)
    def _(b):
        acc[b] = jnp.zeros((block, width), F32)

    @pl.loop(0, groups)
    def _(g):
        got_copy(g).wait()
        shares = []
        for d in range(group):
            src = g * group + d
            for k in range(slots):
                col = cols_ref[k, src]
                acc[col] += got[src, k * block : (k + 1) * block, :].astype(F32)
            extra = got[src, slots * block : slots * block + EXTRA, :].astype(F32)
            shares.append(extra[:2] + extra[2:4])
        shares = [shares[place] for place in places]
        at = pl.ds(pl.multiple_of(g * group, group), group)
        gw[at, :width] = jnp.concatenate([share[:1] for share in shares], axis=0)
        gw[at, width:] = jnp.concatenate([share[1:] for share in shares], axis=0)

    load.wait()

    @pl.loop(0, parts)
    def _(p):
        for b in range(part):
            at = p * part + b
            out[at] = (base[at] + acc[at]).astype(BF16)
        out_copy(p).start()

    gs_ref[...] = gw[:, :width].T
    gn_ref[...] = gw[:, width:].T
    for p in range(parts):
        out_copy(p).wait()


def last_sum(cols, got, base, slots, places, parts=4):
    peers, rows, width = got.shape
    blocks, block, _ = base.shape
    groups = peers // len(places)
    hbm = pl.BlockSpec(memory_space=pl.ANY)
    vmem = pl.BlockSpec(memory_space=pltpu.VMEM)
    return pl.pallas_call(
        functools.partial(last_sum_kernel, slots, places, parts),
        in_specs=[pl.BlockSpec(memory_space=pltpu.SMEM), hbm, hbm],
        out_specs=[hbm, vmem, vmem],
        scratch_shapes=[
            pltpu.VMEM((peers, rows, width), BF16),
            pltpu.VMEM((blocks, block, width), BF16),
            pltpu.VMEM((blocks, block, width), F32),
            pltpu.VMEM((blocks, block, width), F32),
            pltpu.VMEM((width, 2 * width), F32),
            pltpu.SemaphoreType.DMA((groups,)),
            pltpu.SemaphoreType.DMA,
            pltpu.SemaphoreType.DMA((parts,)),
        ],
        out_shape=[
            jax.ShapeDtypeStruct((blocks, block, width), BF16),
            jax.ShapeDtypeStruct((width, width), F32),
            jax.ShapeDtypeStruct((width, width), F32),
        ],
        compiler_params=pltpu.CompilerParams(vmem_limit_bytes=FULL_VMEM),
        cost_estimate=cost(peers * rows * width, 2 * peers * rows * width + 6 * blocks * block * width),
        name="last_sum",
    )(cols, got, base)


def exchange(x):
    return lax.all_to_all(x, ("z", "gy", "core"), split_axis=0, concat_axis=0, tiled=True)


def body(
    grad_out,
    preact,
    features,
    neighbour_mean,
    w_self,
    w_neigh,
    degrees,
    tile_values,
    tile_list,
    send_counts,
):
    nodes, width = grad_out.shape
    block = tile_values.shape[1]
    cores = lax.axis_size("core")
    group = cores * lax.axis_size("gy")
    peers = lax.axis_size("z") * group
    places = order(group, cores)
    capacity = tile_values.shape[0] // peers
    scale = 1.0 / math.sqrt(nodes * peers)
    slot_list = tile_list[0]
    tiles = tile_values.reshape(peers, capacity, block, block)
    last = capacity - 1

    degrees = degrees.reshape(nodes // block, block)
    sent1 = first_stage(
        slot_list, send_counts, degrees, w_neigh, grad_out, preact, features, neighbour_mean,
        tiles, last, scale, places,
    )
    got1 = exchange(sent1)
    grad_neighbour, st = node_stage(grad_out, preact, w_neigh, degrees)
    sent2 = terms(slot_list, send_counts, st, tiles, tuple(range(last)), places)

    extra = got1[:, block : block + EXTRA, :]
    share = jnp.sum(extra[:, :4, :].astype(F32), axis=0)
    share = share[:2] + share[2:]
    high = lax.reduce_precision(share, exponent_bits=8, mantissa_bits=7)
    low = share - high
    pay = jnp.concatenate([high, low, jnp.zeros((EXTRA - 4, width), F32)], axis=0).astype(BF16)
    sent2 = lax.dynamic_update_slice(
        sent2, jnp.broadcast_to(pay[None], (peers, EXTRA, width)), (0, last * block, 0)
    )
    got2 = exchange(sent2)
    cols = extra[:, 4, :8].astype(jnp.int32).T
    base = first_sum(cols, got1, grad_out, preact, w_self)
    grad_features, grad_w_self, grad_w_neigh = last_sum(cols, got2, base, last, places)
    return (grad_features.reshape(nodes, width), grad_neighbour, grad_w_self, grad_w_neigh)


def solution(mesh):
    major, minor = mesh.devices.shape
    mesh = jax.sharding.Mesh(mesh.devices.reshape(major // CORES, CORES, minor), AXES)
    placed = (
        P(AXES, None),
        P(AXES, None),
        P(AXES, None),
        P(AXES, None),
        P(),
        P(),
        P(AXES),
        P(AXES, None, None),
        P(AXES, None, None),
        P(AXES, None),
    )
    return jax.shard_map(
        body,
        mesh=mesh,
        in_specs=placed,
        out_specs=(P(AXES, None), P(AXES, None), P(), P()),
        check_vma=False,
    )
```

```python
import functools
import math

import jax
import jax.numpy as jnp
from jax import lax
from jax.experimental import pallas as pl
from jax.experimental.pallas import tpu as pltpu
from jax.sharding import PartitionSpec as P

BF16 = jnp.bfloat16
F32 = jnp.float32
CORES = 2
AXES = ("z", "core", "gy")
NT = (((1,), (1,)), ((), ()))
TN = (((0,), (0,)), ((), ()))
VMEM_LIMIT = 50 * 1024 * 1024
FULL_VMEM = 60 * 1024 * 1024
EXTRA = 8


def dot(a, b, dims=(((1,), (0,)), ((), ()))):
    return lax.dot_general(a, b, dims, preferred_element_type=F32)


def params():
    return pltpu.CompilerParams(
        dimension_semantics=("arbitrary",), vmem_limit_bytes=VMEM_LIMIT
    )


def cost(flops, nbytes):
    return pl.CostEstimate(flops=flops, bytes_accessed=nbytes, transcendentals=0)


def local(index, blocks):
    return index & (blocks - 1) if blocks & (blocks - 1) == 0 else lax.rem(index, blocks)


def order(group, cores):
    return [d % (group // cores) * cores + d // (group // cores) for d in range(group)]


def relu_of(grad_ref, pre_ref):
    grad = grad_ref[...]
    return jnp.where(pre_ref[...] > 0, grad, jnp.zeros_like(grad))


def scaled_rows(wn, relu_t, deg, st_ref, at):
    block = deg.shape[1]
    ngt = dot(wn, relu_t)
    inv = 1.0 / deg.astype(F32)
    for b in range(deg.shape[0]):
        st_ref[at + b] = (ngt[:, b * block : (b + 1) * block] * inv[b : b + 1, :]).astype(BF16)


def node_kernel(grad_ref, pre_ref, wn_ref, deg_ref, gn_ref, st_ref):
    relu = relu_of(grad_ref, pre_ref)
    wn = wn_ref[...]
    gn_ref[...] = dot(relu, wn, NT).astype(BF16)
    scaled_rows(wn, relu.T, deg_ref[...], st_ref, 0)


def node_stage(grad_out, preact, w_neigh, degrees):
    rows, width = grad_out.shape
    blocks, block = degrees.shape
    tile = 8 * block
    node = pl.BlockSpec((tile, width), lambda i: (i, 0))
    return pl.pallas_call(
        node_kernel,
        grid=(rows // tile,),
        in_specs=[
            node,
            node,
            pl.BlockSpec((width, width), lambda i: (0, 0)),
            pl.BlockSpec((8, block), lambda i: (i, 0)),
        ],
        out_specs=[node, pl.BlockSpec((8, width, block), lambda i: (i, 0, 0))],
        out_shape=[
            jax.ShapeDtypeStruct((rows, width), BF16),
            jax.ShapeDtypeStruct((blocks, width, block), BF16),
        ],
        compiler_params=params(),
        cost_estimate=cost(4 * rows * width * width, 8 * rows * width),
        name="node_stage",
    )(grad_out, preact, w_neigh, degrees)


def hi_lo_rows(a, b, tail):
    width = a.shape[1]
    row = lax.broadcasted_iota(jnp.int32, (EXTRA, width), 0)
    a = jnp.broadcast_to(a, (EXTRA, width))
    b = jnp.broadcast_to(b, (EXTRA, width))
    a_hi = a.astype(BF16).astype(F32)
    b_hi = b.astype(BF16).astype(F32)
    out = jnp.where(row == 0, a_hi, jnp.where(row == 1, b_hi, jnp.where(row == 2, a - a_hi, b - b_hi)))
    return jnp.where(row < 4, out, jnp.where(row == 4, tail, 0.0))


def term_rows(slots, capacity, places, step, list_ref, count_ref, st_ref, tile_ref, out_ref, at, transposed, share):
    blocks, width, _ = st_ref.shape
    base = len(slots) * width
    for d, place in enumerate(places):
        dest = step * len(places) + d
        for k, slot in enumerate(slots):
            rows_t = st_ref[local(list_ref[0, dest * capacity + slot], blocks)]
            if transposed:
                term = dot(rows_t, tile_ref[at + d, k])
            else:
                term = dot(tile_ref[at + d, k], rows_t, (((0,), (1,)), ((), ())))
            keep = slot < count_ref[0, dest]
            out_ref[at + place, k * width : (k + 1) * width, :] = jnp.where(keep, term, 0.0).astype(BF16)
        if share is None:
            extra = jnp.zeros((EXTRA, width), BF16)
        else:
            lane = lax.broadcasted_iota(jnp.int32, (1, width), 1)
            cols = jnp.zeros((1, width), jnp.int32)
            for c in range(capacity):
                cols = jnp.where(lane == c, local(list_ref[1, dest * capacity + c], blocks), cols)
            extra = hi_lo_rows(
                share[d : d + 1, :width],
                share[d : d + 1, width:],
                jnp.broadcast_to(cols.astype(F32), (EXTRA, width)),
            ).astype(BF16)
        out_ref[at + place, base : base + EXTRA, :] = extra


def term_kernel(slots, capacity, places, list_ref, count_ref, st_ref, tile_ref, out_ref):
    step = pl.program_id(0)
    term_rows(slots, capacity, places, step, list_ref, count_ref, st_ref, tile_ref, out_ref, 0, False, None)


def terms(tile_list, counts, st, tiles, slots, places):
    peers, capacity, block, _ = tiles.shape
    blocks, width, _ = st.shape
    n = len(slots)
    at = slots[0] // n
    group = len(places)
    rows = n * block + EXTRA
    return pl.pallas_call(
        functools.partial(term_kernel, slots, capacity, places),
        grid_spec=pltpu.PrefetchScalarGridSpec(
            num_scalar_prefetch=2,
            grid=(peers // group,),
            in_specs=[
                pl.BlockSpec((blocks, width, block), lambda i, *_: (0, 0, 0)),
                pl.BlockSpec((group, n, block, block), lambda i, *_: (i, at, 0, 0)),
            ],
            out_specs=pl.BlockSpec((group, rows, width), lambda i, *_: (i, 0, 0)),
        ),
        out_shape=jax.ShapeDtypeStruct((peers, rows, width), BF16),
        compiler_params=params(),
        cost_estimate=cost(2 * peers * n * block**3, 4 * peers * n * block * block),
        name="terms",
    )(tile_list, counts, st, tiles)


def first_kernel(
    scale, slot, chunks, places,
    list_hbm, count_hbm, deg_hbm, wn_hbm, grad_hbm, pre_hbm, feat_hbm, mean_hbm, tile_hbm,
    out_hbm,
    list_ref, count_ref, deg_ref, wn_ref, grad_ref, pre_ref, feat_ref, mean_ref, tile_ref, out_ref, st_ref, gw_ref, relu_ref,
    small_sem, node_sem, tile_sem, out_sem,
):
    nodes, width = grad_ref.shape
    peers, capacity = tile_hbm.shape[:2]
    part = nodes // chunks
    group = len(places)
    groups = peers // group
    small = [
        pltpu.make_async_copy(src, dst, small_sem.at[i])
        for i, (src, dst) in enumerate(
            ((wn_hbm, wn_ref), (deg_hbm, deg_ref), (list_hbm, list_ref), (count_hbm, count_ref))
        )
    ]
    pairs = ((grad_hbm, grad_ref), (pre_hbm, pre_ref), (feat_hbm, feat_ref), (mean_hbm, mean_ref))

    def node_copies(c):
        at = pl.ds(pl.multiple_of(c * part, part), part)
        return [
            pltpu.make_async_copy(src.at[at], dst.at[at], node_sem.at[i, c])
            for i, (src, dst) in enumerate(pairs)
        ]

    def tile_copy(g):
        at = pl.ds(g * group, group)
        return pltpu.make_async_copy(tile_hbm.at[at, slot : slot + 1], tile_ref.at[at], tile_sem.at[g])

    def out_copy(g):
        at = pl.ds(g * group, group)
        return pltpu.make_async_copy(out_ref.at[at], out_hbm.at[at], out_sem.at[g])

    for copy in small[:2]:
        copy.start()
    for half in (slice(0, 2), slice(2, 4)):
        for c in range(chunks):
            for copy in node_copies(c)[half]:
                copy.start()
    for copy in small[2:]:
        copy.start()
    for g in range(groups):
        tile_copy(g).start()
    gw_ref[...] = jnp.zeros_like(gw_ref)
    for copy in small[:2]:
        copy.wait()

    @pl.loop(0, chunks)
    def _(c):
        for copy in node_copies(c)[:2]:
            copy.wait()
        at = pl.ds(pl.multiple_of(c * part, part), part)
        relu_t = relu_of(grad_ref.at[at], pre_ref.at[at]).T
        relu_ref[c] = relu_t
        rows = part // deg_ref.shape[1]
        deg = deg_ref[pl.ds(pl.multiple_of(c * rows, rows), rows), :]
        scaled_rows(wn_ref[...], relu_t, deg, st_ref, c * rows)

    @pl.loop(0, chunks)
    def _(c):
        for copy in node_copies(c)[2:]:
            copy.wait()
        at = pl.ds(pl.multiple_of(c * part, part), part)
        relu_t = relu_ref[c]
        gw_ref[:, :width] += dot(relu_t, feat_ref[at, :]) * scale
        gw_ref[:, width:] += dot(relu_t, mean_ref[at, :]) * scale

    for copy in small[2:]:
        copy.wait()

    @pl.loop(0, groups)
    def _(g):
        tile_copy(g).wait()
        share = gw_ref[pl.ds(pl.multiple_of(g * group, group), group), :]
        term_rows(
            (slot,), capacity, places, g, list_ref, count_ref, st_ref,
            tile_ref, out_ref, g * group, True, share,
        )
        out_copy(g).start()

    for g in range(groups):
        out_copy(g).wait()


def first_stage(tile_list, counts, degrees, w_neigh, grad_out, preact, features, mean, tiles, slot, scale, places, chunks=2):
    nodes, width = grad_out.shape
    peers, capacity, block, _ = tiles.shape
    blocks = nodes // block
    rows = block + EXTRA
    groups = peers // len(places)
    hbm = pl.BlockSpec(memory_space=pl.ANY)
    node = pltpu.VMEM((nodes, width), BF16)
    return pl.pallas_call(
        functools.partial(first_kernel, scale, slot, chunks, places),
        in_specs=[hbm] * 9,
        out_specs=hbm,
        out_shape=jax.ShapeDtypeStruct((peers, rows, width), BF16),
        scratch_shapes=[
            pltpu.SMEM(tile_list.shape, jnp.int32),
            pltpu.SMEM(counts.shape, jnp.int32),
            pltpu.VMEM(degrees.shape, jnp.int32),
            pltpu.VMEM(w_neigh.shape, BF16),
            node,
            node,
            node,
            node,
            pltpu.VMEM((peers, 1, block, block), BF16),
            pltpu.VMEM((peers, rows, width), BF16),
            pltpu.VMEM((blocks, width, block), BF16),
            pltpu.VMEM((width, 2 * width), F32),
            pltpu.VMEM((chunks, width, nodes // chunks), BF16),
            pltpu.SemaphoreType.DMA((4,)),
            pltpu.SemaphoreType.DMA((4, chunks)),
            pltpu.SemaphoreType.DMA((groups,)),
            pltpu.SemaphoreType.DMA((groups,)),
        ],
        compiler_params=pltpu.CompilerParams(vmem_limit_bytes=FULL_VMEM),
        cost_estimate=cost(6 * nodes * width * width + 2 * peers * block**3, 8 * nodes * width + 4 * peers * block * block),
        name="first_stage",
    )(tile_list, counts, degrees, w_neigh, grad_out, preact, features, mean, tiles)


def first_sum_kernel(group, cols_ref, got_ref, grad_ref, pre_ref, ws_ref, out_ref, acc):
    step = pl.program_id(0)
    steps = pl.num_programs(0)
    block = acc.shape[1]

    @pl.when(step == 0)
    def _():
        acc[...] = jnp.zeros_like(acc)

    for d in range(group):
        col = cols_ref[2, step * group + d]
        acc[col] += got_ref[d, :block, :].astype(F32)

    @pl.when(step == steps - 1)
    def _():
        @pl.loop(0, acc.shape[0])
        def _(b):
            at = pl.ds(pl.multiple_of(b * block, block), block)
            relu = relu_of(grad_ref.at[at], pre_ref.at[at])
            out_ref[b] = acc[b].T + dot(relu, ws_ref[...], NT)


def first_sum(cols, got, grad_out, preact, w_self, group=8):
    peers, rows, width = got.shape
    nodes = grad_out.shape[0]
    block = rows - EXTRA
    blocks = nodes // block
    whole = pl.BlockSpec((nodes, width), lambda i, *_: (0, 0))
    return pl.pallas_call(
        functools.partial(first_sum_kernel, group),
        grid_spec=pltpu.PrefetchScalarGridSpec(
            num_scalar_prefetch=1,
            grid=(peers // group,),
            in_specs=[
                pl.BlockSpec((group, rows, width), lambda i, *_: (i, 0, 0)),
                whole,
                whole,
                pl.BlockSpec((width, width), lambda i, *_: (0, 0)),
            ],
            out_specs=pl.BlockSpec((blocks, block, width), lambda i, *_: (0, 0, 0)),
            scratch_shapes=[pltpu.VMEM((blocks, block, width), F32)],
        ),
        out_shape=jax.ShapeDtypeStruct((blocks, block, width), F32),
        compiler_params=params(),
        cost_estimate=cost(2 * nodes * width * width, 2 * peers * rows * width + 8 * nodes * width),
        name="first_sum",
    )(cols, got, grad_out, preact, w_self)


def last_sum_kernel(
    slots, places, parts, cols_ref, got_hbm, base_hbm, out_hbm, gs_ref, gn_ref,
    got, out, base, acc, gw, got_sem, base_sem, out_sem,
):
    peers = got.shape[0]
    blocks, block, width = acc.shape
    group = len(places)
    groups = peers // group
    part = blocks // parts

    def got_copy(g):
        at = pl.ds(g * group, group)
        return pltpu.make_async_copy(got_hbm.at[at], got.at[at], got_sem.at[g])

    def out_copy(p):
        at = pl.ds(p * part, part)
        return pltpu.make_async_copy(out.at[at], out_hbm.at[at], out_sem.at[p])

    load = pltpu.make_async_copy(base_hbm, base, base_sem)
    for g in range(groups):
        got_copy(g).start()
    load.start()

    @pl.loop(0, blocks, unroll=4)
    def _(b):
        acc[b] = jnp.zeros((block, width), F32)

    @pl.loop(0, groups)
    def _(g):
        got_copy(g).wait()
        shares = []
        for d in range(group):
            src = g * group + d
            for k in range(slots):
                col = cols_ref[k, src]
                acc[col] += got[src, k * block : (k + 1) * block, :].astype(F32)
            extra = got[src, slots * block : slots * block + EXTRA, :].astype(F32)
            shares.append(extra[:2] + extra[2:4])
        shares = [shares[place] for place in places]
        at = pl.ds(pl.multiple_of(g * group, group), group)
        gw[at, :width] = jnp.concatenate([share[:1] for share in shares], axis=0)
        gw[at, width:] = jnp.concatenate([share[1:] for share in shares], axis=0)

    load.wait()

    @pl.loop(0, parts)
    def _(p):
        for b in range(part):
            at = p * part + b
            out[at] = (base[at] + acc[at]).astype(BF16)
        out_copy(p).start()

    gs_ref[...] = gw[:, :width].T
    gn_ref[...] = gw[:, width:].T
    for p in range(parts):
        out_copy(p).wait()


def last_sum(cols, got, base, slots, places, parts=4):
    peers, rows, width = got.shape
    blocks, block, _ = base.shape
    groups = peers // len(places)
    hbm = pl.BlockSpec(memory_space=pl.ANY)
    vmem = pl.BlockSpec(memory_space=pltpu.VMEM)
    return pl.pallas_call(
        functools.partial(last_sum_kernel, slots, places, parts),
        in_specs=[pl.BlockSpec(memory_space=pltpu.SMEM), hbm, hbm],
        out_specs=[hbm, vmem, vmem],
        scratch_shapes=[
            pltpu.VMEM((peers, rows, width), BF16),
            pltpu.VMEM((blocks, block, width), BF16),
            pltpu.VMEM((blocks, block, width), F32),
            pltpu.VMEM((blocks, block, width), F32),
            pltpu.VMEM((width, 2 * width), F32),
            pltpu.SemaphoreType.DMA((groups,)),
            pltpu.SemaphoreType.DMA,
            pltpu.SemaphoreType.DMA((parts,)),
        ],
        out_shape=[
            jax.ShapeDtypeStruct((blocks, block, width), BF16),
            jax.ShapeDtypeStruct((width, width), F32),
            jax.ShapeDtypeStruct((width, width), F32),
        ],
        compiler_params=pltpu.CompilerParams(vmem_limit_bytes=FULL_VMEM),
        cost_estimate=cost(peers * rows * width, 2 * peers * rows * width + 6 * blocks * block * width),
        name="last_sum",
    )(cols, got, base)


def exchange(x):
    return lax.all_to_all(x, ("z", "gy", "core"), split_axis=0, concat_axis=0, tiled=True)


def body(
    grad_out,
    preact,
    features,
    neighbour_mean,
    w_self,
    w_neigh,
    degrees,
    tile_values,
    tile_list,
    send_counts,
):
    nodes, width = grad_out.shape
    block = tile_values.shape[1]
    cores = lax.axis_size("core")
    group = cores * lax.axis_size("gy")
    peers = lax.axis_size("z") * group
    places = order(group, cores)
    capacity = tile_values.shape[0] // peers
    scale = 1.0 / math.sqrt(nodes * peers)
    slot_list = tile_list[0]
    tiles = tile_values.reshape(peers, capacity, block, block)
    last = capacity - 1

    degrees = degrees.reshape(nodes // block, block)
    sent1 = first_stage(
        slot_list, send_counts, degrees, w_neigh, grad_out, preact, features, neighbour_mean,
        tiles, last, scale, places + [group + place for place in places],
    )
    got1 = exchange(sent1)
    grad_neighbour, st = node_stage(grad_out, preact, w_neigh, degrees)
    sent2 = terms(slot_list, send_counts, st, tiles, tuple(range(last)), places)

    extra = got1[:, block : block + EXTRA, :]
    share = jnp.sum(extra[:, :4, :].astype(F32), axis=0)
    share = share[:2] + share[2:]
    high = lax.reduce_precision(share, exponent_bits=8, mantissa_bits=7)
    low = share - high
    pay = jnp.concatenate([high, low, jnp.zeros((EXTRA - 4, width), F32)], axis=0).astype(BF16)
    sent2 = lax.dynamic_update_slice(
        sent2, jnp.broadcast_to(pay[None], (peers, EXTRA, width)), (0, last * block, 0)
    )
    got2 = exchange(sent2)
    cols = extra[:, 4, :8].astype(jnp.int32).T
    base = first_sum(cols, got1, grad_out, preact, w_self)
    grad_features, grad_w_self, grad_w_neigh = last_sum(cols, got2, base, last, places)
    return (grad_features.reshape(nodes, width), grad_neighbour, grad_w_self, grad_w_neigh)


def solution(mesh):
    major, minor = mesh.devices.shape
    mesh = jax.sharding.Mesh(mesh.devices.reshape(major // CORES, CORES, minor), AXES)
    placed = (
        P(AXES, None),
        P(AXES, None),
        P(AXES, None),
        P(AXES, None),
        P(),
        P(),
        P(AXES),
        P(AXES, None, None),
        P(AXES, None, None),
        P(AXES, None),
    )
    return jax.shard_map(
        body,
        mesh=mesh,
        in_specs=placed,
        out_specs=(P(AXES, None), P(AXES, None), P(), P()),
        check_vma=False,
    )
```

```python
import functools
import math

import jax
import jax.numpy as jnp
from jax import lax
from jax.experimental import pallas as pl
from jax.experimental.pallas import tpu as pltpu
from jax.sharding import PartitionSpec as P

BF16 = jnp.bfloat16
F32 = jnp.float32
CORES = 2
AXES = ("z", "core", "gy")
NT = (((1,), (1,)), ((), ()))
TN = (((0,), (0,)), ((), ()))
VMEM_LIMIT = 50 * 1024 * 1024
FULL_VMEM = 60 * 1024 * 1024
EXTRA = 8


def dot(a, b, dims=(((1,), (0,)), ((), ()))):
    return lax.dot_general(a, b, dims, preferred_element_type=F32)


def params():
    return pltpu.CompilerParams(
        dimension_semantics=("arbitrary",), vmem_limit_bytes=VMEM_LIMIT
    )


def cost(flops, nbytes):
    return pl.CostEstimate(flops=flops, bytes_accessed=nbytes, transcendentals=0)


def local(index, blocks):
    return index & (blocks - 1) if blocks & (blocks - 1) == 0 else lax.rem(index, blocks)


def order(group, cores):
    return [d % (group // cores) * cores + d // (group // cores) for d in range(group)]


def relu_of(grad_ref, pre_ref):
    grad = grad_ref[...]
    return jnp.where(pre_ref[...] > 0, grad, jnp.zeros_like(grad))


def scaled_rows(wn, relu_t, deg, st_ref, at):
    block = deg.shape[1]
    ngt = dot(wn, relu_t)
    inv = 1.0 / deg.astype(F32)
    for b in range(deg.shape[0]):
        st_ref[at + b] = (ngt[:, b * block : (b + 1) * block] * inv[b : b + 1, :]).astype(BF16)


def node_kernel(grad_ref, pre_ref, wn_ref, deg_ref, gn_ref, st_ref):
    relu = relu_of(grad_ref, pre_ref)
    wn = wn_ref[...]
    gn_ref[...] = dot(relu, wn, NT).astype(BF16)
    scaled_rows(wn, relu.T, deg_ref[...], st_ref, 0)


def node_stage(grad_out, preact, w_neigh, degrees):
    rows, width = grad_out.shape
    blocks, block = degrees.shape
    tile = 8 * block
    node = pl.BlockSpec((tile, width), lambda i: (i, 0))
    return pl.pallas_call(
        node_kernel,
        grid=(rows // tile,),
        in_specs=[
            node,
            node,
            pl.BlockSpec((width, width), lambda i: (0, 0)),
            pl.BlockSpec((8, block), lambda i: (i, 0)),
        ],
        out_specs=[node, pl.BlockSpec((8, width, block), lambda i: (i, 0, 0))],
        out_shape=[
            jax.ShapeDtypeStruct((rows, width), BF16),
            jax.ShapeDtypeStruct((blocks, width, block), BF16),
        ],
        compiler_params=params(),
        cost_estimate=cost(4 * rows * width * width, 8 * rows * width),
        name="node_stage",
    )(grad_out, preact, w_neigh, degrees)


def hi_lo_rows(a, b, tail):
    width = a.shape[1]
    row = lax.broadcasted_iota(jnp.int32, (EXTRA, width), 0)
    a = jnp.broadcast_to(a, (EXTRA, width))
    b = jnp.broadcast_to(b, (EXTRA, width))
    a_hi = a.astype(BF16).astype(F32)
    b_hi = b.astype(BF16).astype(F32)
    out = jnp.where(row == 0, a_hi, jnp.where(row == 1, b_hi, jnp.where(row == 2, a - a_hi, b - b_hi)))
    return jnp.where(row < 4, out, jnp.where(row == 4, tail, 0.0))


def term_rows(slots, capacity, places, step, list_ref, count_ref, st_ref, tile_ref, out_ref, at, transposed, share):
    blocks, width, _ = st_ref.shape
    base = len(slots) * width
    for d, place in enumerate(places):
        dest = step * len(places) + d
        for k, slot in enumerate(slots):
            rows_t = st_ref[local(list_ref[0, dest * capacity + slot], blocks)]
            if transposed:
                term = dot(rows_t, tile_ref[at + d, k])
            else:
                term = dot(tile_ref[at + d, k], rows_t, (((0,), (1,)), ((), ())))
            keep = slot < count_ref[0, dest]
            out_ref[at + place, k * width : (k + 1) * width, :] = jnp.where(keep, term, 0.0).astype(BF16)
        if share is None:
            extra = jnp.zeros((EXTRA, width), BF16)
        else:
            lane = lax.broadcasted_iota(jnp.int32, (1, width), 1)
            cols = jnp.zeros((1, width), jnp.int32)
            for c in range(capacity):
                cols = jnp.where(lane == c, local(list_ref[1, dest * capacity + c], blocks), cols)
            extra = hi_lo_rows(
                share[d : d + 1, :width],
                share[d : d + 1, width:],
                jnp.broadcast_to(cols.astype(F32), (EXTRA, width)),
            ).astype(BF16)
        out_ref[at + place, base : base + EXTRA, :] = extra


def term_kernel(slots, capacity, places, list_ref, count_ref, st_ref, tile_ref, out_ref):
    step = pl.program_id(0)
    term_rows(slots, capacity, places, step, list_ref, count_ref, st_ref, tile_ref, out_ref, 0, False, None)


def terms(tile_list, counts, st, tiles, slots, places):
    peers, capacity, block, _ = tiles.shape
    blocks, width, _ = st.shape
    n = len(slots)
    at = slots[0] // n
    group = len(places)
    rows = n * block + EXTRA
    return pl.pallas_call(
        functools.partial(term_kernel, slots, capacity, places),
        grid_spec=pltpu.PrefetchScalarGridSpec(
            num_scalar_prefetch=2,
            grid=(peers // group,),
            in_specs=[
                pl.BlockSpec((blocks, width, block), lambda i, *_: (0, 0, 0)),
                pl.BlockSpec((group, n, block, block), lambda i, *_: (i, at, 0, 0)),
            ],
            out_specs=pl.BlockSpec((group, rows, width), lambda i, *_: (i, 0, 0)),
        ),
        out_shape=jax.ShapeDtypeStruct((peers, rows, width), BF16),
        compiler_params=params(),
        cost_estimate=cost(2 * peers * n * block**3, 4 * peers * n * block * block),
        name="terms",
    )(tile_list, counts, st, tiles)


def first_kernel(
    scale, slot, chunks, places,
    list_hbm, count_hbm, deg_hbm, wn_hbm, grad_hbm, pre_hbm, feat_hbm, mean_hbm, tile_hbm,
    out_hbm,
    list_ref, count_ref, deg_ref, wn_ref, grad_ref, pre_ref, feat_ref, mean_ref, tile_ref, out_ref, st_ref, gw_ref, relu_ref,
    small_sem, node_sem, tile_sem, out_sem,
):
    nodes, width = grad_ref.shape
    peers, capacity = tile_hbm.shape[:2]
    part = nodes // chunks
    group = len(places)
    groups = peers // group
    small = [
        pltpu.make_async_copy(src, dst, small_sem.at[i])
        for i, (src, dst) in enumerate(
            ((wn_hbm, wn_ref), (deg_hbm, deg_ref), (list_hbm, list_ref), (count_hbm, count_ref))
        )
    ]
    pairs = ((grad_hbm, grad_ref), (pre_hbm, pre_ref), (feat_hbm, feat_ref), (mean_hbm, mean_ref))

    def node_copies(c):
        at = pl.ds(pl.multiple_of(c * part, part), part)
        return [
            pltpu.make_async_copy(src.at[at], dst.at[at], node_sem.at[i, c])
            for i, (src, dst) in enumerate(pairs)
        ]

    def tile_copy(g):
        at = pl.ds(g * group, group)
        return pltpu.make_async_copy(tile_hbm.at[at, slot : slot + 1], tile_ref.at[at], tile_sem.at[g])

    def out_copy(g):
        at = pl.ds(g * group, group)
        return pltpu.make_async_copy(out_ref.at[at], out_hbm.at[at], out_sem.at[g])

    for copy in small[:2]:
        copy.start()
    for half in (slice(0, 2), slice(2, 4)):
        for c in range(chunks):
            for copy in node_copies(c)[half]:
                copy.start()
    for copy in small[2:]:
        copy.start()
    for g in range(groups):
        tile_copy(g).start()
    gw_ref[...] = jnp.zeros_like(gw_ref)
    for copy in small[:2]:
        copy.wait()

    @pl.loop(0, chunks)
    def _(c):
        for copy in node_copies(c)[:2]:
            copy.wait()
        at = pl.ds(pl.multiple_of(c * part, part), part)
        relu_t = relu_of(grad_ref.at[at], pre_ref.at[at]).T
        relu_ref[c] = relu_t
        rows = part // deg_ref.shape[1]
        deg = deg_ref[pl.ds(pl.multiple_of(c * rows, rows), rows), :]
        scaled_rows(wn_ref[...], relu_t, deg, st_ref, c * rows)

    @pl.loop(0, chunks)
    def _(c):
        for copy in node_copies(c)[2:]:
            copy.wait()
        at = pl.ds(pl.multiple_of(c * part, part), part)
        relu_t = relu_ref[c]
        gw_ref[:, :width] += dot(relu_t, feat_ref[at, :]) * scale
        gw_ref[:, width:] += dot(relu_t, mean_ref[at, :]) * scale

    for copy in small[2:]:
        copy.wait()

    @pl.loop(0, groups)
    def _(g):
        tile_copy(g).wait()
        share = gw_ref[pl.ds(pl.multiple_of(g * group, group), group), :]
        term_rows(
            (slot,), capacity, places, g, list_ref, count_ref, st_ref,
            tile_ref, out_ref, g * group, True, share,
        )
        out_copy(g).start()

    for g in range(groups):
        out_copy(g).wait()


def first_stage(tile_list, counts, degrees, w_neigh, grad_out, preact, features, mean, tiles, slot, scale, places, chunks=2):
    nodes, width = grad_out.shape
    peers, capacity, block, _ = tiles.shape
    blocks = nodes // block
    rows = block + EXTRA
    groups = peers // len(places)
    hbm = pl.BlockSpec(memory_space=pl.ANY)
    node = pltpu.VMEM((nodes, width), BF16)
    return pl.pallas_call(
        functools.partial(first_kernel, scale, slot, chunks, places),
        in_specs=[hbm] * 9,
        out_specs=hbm,
        out_shape=jax.ShapeDtypeStruct((peers, rows, width), BF16),
        scratch_shapes=[
            pltpu.SMEM(tile_list.shape, jnp.int32),
            pltpu.SMEM(counts.shape, jnp.int32),
            pltpu.VMEM(degrees.shape, jnp.int32),
            pltpu.VMEM(w_neigh.shape, BF16),
            node,
            node,
            node,
            node,
            pltpu.VMEM((peers, 1, block, block), BF16),
            pltpu.VMEM((peers, rows, width), BF16),
            pltpu.VMEM((blocks, width, block), BF16),
            pltpu.VMEM((width, 2 * width), F32),
            pltpu.VMEM((chunks, width, nodes // chunks), BF16),
            pltpu.SemaphoreType.DMA((4,)),
            pltpu.SemaphoreType.DMA((4, chunks)),
            pltpu.SemaphoreType.DMA((groups,)),
            pltpu.SemaphoreType.DMA((groups,)),
        ],
        compiler_params=pltpu.CompilerParams(vmem_limit_bytes=FULL_VMEM),
        cost_estimate=cost(6 * nodes * width * width + 2 * peers * block**3, 8 * nodes * width + 4 * peers * block * block),
        name="first_stage",
    )(tile_list, counts, degrees, w_neigh, grad_out, preact, features, mean, tiles)


def first_sum_kernel(group, cols_ref, got_ref, grad_ref, pre_ref, ws_ref, out_ref, acc):
    step = pl.program_id(0)
    steps = pl.num_programs(0)
    block = acc.shape[1]

    @pl.when(step == 0)
    def _():
        acc[...] = jnp.zeros_like(acc)

    for d in range(group):
        col = cols_ref[2, step * group + d]
        acc[col] += got_ref[d, :block, :].astype(F32)

    @pl.when(step == steps - 1)
    def _():
        @pl.loop(0, acc.shape[0])
        def _(b):
            at = pl.ds(pl.multiple_of(b * block, block), block)
            relu = relu_of(grad_ref.at[at], pre_ref.at[at])
            out_ref[b] = acc[b].T + dot(relu, ws_ref[...], NT)


def first_sum(cols, got, grad_out, preact, w_self, group=8):
    peers, rows, width = got.shape
    nodes = grad_out.shape[0]
    block = rows - EXTRA
    blocks = nodes // block
    whole = pl.BlockSpec((nodes, width), lambda i, *_: (0, 0))
    return pl.pallas_call(
        functools.partial(first_sum_kernel, group),
        grid_spec=pltpu.PrefetchScalarGridSpec(
            num_scalar_prefetch=1,
            grid=(peers // group,),
            in_specs=[
                pl.BlockSpec((group, rows, width), lambda i, *_: (i, 0, 0)),
                whole,
                whole,
                pl.BlockSpec((width, width), lambda i, *_: (0, 0)),
            ],
            out_specs=pl.BlockSpec((blocks, block, width), lambda i, *_: (0, 0, 0)),
            scratch_shapes=[pltpu.VMEM((blocks, block, width), F32)],
        ),
        out_shape=jax.ShapeDtypeStruct((blocks, block, width), F32),
        compiler_params=params(),
        cost_estimate=cost(2 * nodes * width * width, 2 * peers * rows * width + 8 * nodes * width),
        name="first_sum",
    )(cols, got, grad_out, preact, w_self)


def last_sum_kernel(
    slots, places, parts, cols_hbm, got_hbm, base_hbm, out_hbm, gs_ref, gn_ref,
    cols_ref, got, out, base, acc, gw, cols_sem, got_sem, base_sem, out_sem,
):
    peers = got.shape[0]
    blocks, block, width = acc.shape
    group = len(places)
    groups = peers // group
    part = blocks // parts

    def got_copy(g):
        at = pl.ds(g * group, group)
        return pltpu.make_async_copy(got_hbm.at[at], got.at[at], got_sem.at[g])

    def out_copy(p):
        at = pl.ds(p * part, part)
        return pltpu.make_async_copy(out.at[at], out_hbm.at[at], out_sem.at[p])

    load = pltpu.make_async_copy(base_hbm, base, base_sem)
    cols_load = pltpu.make_async_copy(cols_hbm, cols_ref, cols_sem)
    cols_load.start()
    for g in range(groups):
        got_copy(g).start()
    load.start()

    @pl.loop(0, blocks, unroll=4)
    def _(b):
        acc[b] = jnp.zeros((block, width), F32)

    cols_load.wait()

    @pl.loop(0, groups)
    def _(g):
        got_copy(g).wait()
        shares = []
        for d in range(group):
            src = g * group + d
            for k in range(slots):
                col = cols_ref[k, src]
                acc[col] += got[src, k * block : (k + 1) * block, :].astype(F32)
            extra = got[src, slots * block : slots * block + EXTRA, :].astype(F32)
            shares.append(extra[:2] + extra[2:4])
        shares = [shares[place] for place in places]
        at = pl.ds(pl.multiple_of(g * group, group), group)
        gw[at, :width] = jnp.concatenate([share[:1] for share in shares], axis=0)
        gw[at, width:] = jnp.concatenate([share[1:] for share in shares], axis=0)

    load.wait()

    @pl.loop(0, parts)
    def _(p):
        for b in range(part):
            at = p * part + b
            out[at] = (base[at] + acc[at]).astype(BF16)
        out_copy(p).start()

    gs_ref[...] = gw[:, :width].T
    gn_ref[...] = gw[:, width:].T
    for p in range(parts):
        out_copy(p).wait()


def last_sum(cols, got, base, slots, places, parts=4):
    peers, rows, width = got.shape
    blocks, block, _ = base.shape
    groups = peers // len(places)
    hbm = pl.BlockSpec(memory_space=pl.ANY)
    vmem = pl.BlockSpec(memory_space=pltpu.VMEM)
    return pl.pallas_call(
        functools.partial(last_sum_kernel, slots, places, parts),
        in_specs=[hbm, hbm, hbm],
        out_specs=[hbm, vmem, vmem],
        scratch_shapes=[
            pltpu.SMEM(cols.shape, jnp.int32),
            pltpu.VMEM((peers, rows, width), BF16),
            pltpu.VMEM((blocks, block, width), BF16),
            pltpu.VMEM((blocks, block, width), F32),
            pltpu.VMEM((blocks, block, width), F32),
            pltpu.VMEM((width, 2 * width), F32),
            pltpu.SemaphoreType.DMA,
            pltpu.SemaphoreType.DMA((groups,)),
            pltpu.SemaphoreType.DMA,
            pltpu.SemaphoreType.DMA((parts,)),
        ],
        out_shape=[
            jax.ShapeDtypeStruct((blocks, block, width), BF16),
            jax.ShapeDtypeStruct((width, width), F32),
            jax.ShapeDtypeStruct((width, width), F32),
        ],
        compiler_params=pltpu.CompilerParams(vmem_limit_bytes=FULL_VMEM),
        cost_estimate=cost(peers * rows * width, 2 * peers * rows * width + 6 * blocks * block * width),
        name="last_sum",
    )(cols, got, base)


def exchange(x):
    return lax.all_to_all(x, ("z", "gy", "core"), split_axis=0, concat_axis=0, tiled=True)


def body(
    grad_out,
    preact,
    features,
    neighbour_mean,
    w_self,
    w_neigh,
    degrees,
    tile_values,
    tile_list,
    send_counts,
):
    nodes, width = grad_out.shape
    block = tile_values.shape[1]
    cores = lax.axis_size("core")
    group = cores * lax.axis_size("gy")
    peers = lax.axis_size("z") * group
    places = order(group, cores)
    capacity = tile_values.shape[0] // peers
    scale = 1.0 / math.sqrt(nodes * peers)
    slot_list = tile_list[0]
    tiles = tile_values.reshape(peers, capacity, block, block)
    last = capacity - 1

    degrees = degrees.reshape(nodes // block, block)
    sent1 = first_stage(
        slot_list, send_counts, degrees, w_neigh, grad_out, preact, features, neighbour_mean,
        tiles, last, scale, places + [group + place for place in places],
    )
    got1 = exchange(sent1)
    grad_neighbour, st = node_stage(grad_out, preact, w_neigh, degrees)
    sent2 = terms(slot_list, send_counts, st, tiles, tuple(range(last)), places)

    extra = got1[:, block : block + EXTRA, :]
    share = jnp.sum(extra[:, :4, :].astype(F32), axis=0)
    share = share[:2] + share[2:]
    high = lax.reduce_precision(share, exponent_bits=8, mantissa_bits=7)
    low = share - high
    pay = jnp.concatenate([high, low, jnp.zeros((EXTRA - 4, width), F32)], axis=0).astype(BF16)
    sent2 = lax.dynamic_update_slice(
        sent2, jnp.broadcast_to(pay[None], (peers, EXTRA, width)), (0, last * block, 0)
    )
    got2 = exchange(sent2)
    cols = extra[:, 4, :8].astype(jnp.int32).T
    base = first_sum(cols, got1, grad_out, preact, w_self)
    grad_features, grad_w_self, grad_w_neigh = last_sum(cols, got2, base, last, places)
    return (grad_features.reshape(nodes, width), grad_neighbour, grad_w_self, grad_w_neigh)


def solution(mesh):
    major, minor = mesh.devices.shape
    mesh = jax.sharding.Mesh(mesh.devices.reshape(major // CORES, CORES, minor), AXES)
    placed = (
        P(AXES, None),
        P(AXES, None),
        P(AXES, None),
        P(AXES, None),
        P(),
        P(),
        P(AXES),
        P(AXES, None, None),
        P(AXES, None, None),
        P(AXES, None),
    )
    return jax.shard_map(
        body,
        mesh=mesh,
        in_specs=placed,
        out_specs=(P(AXES, None), P(AXES, None), P(), P()),
        check_vma=False,
    )
```
